256 devices in a mesh: gx: 4 (over z_hi), gy: 8 (over y, core), gz: 8 (over x, z_lo).
Axes of the slice: x: 4, y: 4, z: 8 (z_hi: 4, z_lo: 2; z = z_hi * 2 + z_lo), core: 2. Of those that a mesh axis runs over, the one named last changes fastest.
Arguments:
- inputs: bfloat16 [512, 12288], P(('gx', 'gy'), 'gz'), may hold values from -6 to 6
- w_in: bfloat16 [12288, 24576], P('gz', ('gx', 'gy')), may hold values from -0.0546875 to 0.0546875
- w_out: bfloat16 [24576, 12288], P(('gx', 'gy'), 'gz'), may hold values from -0.0390625 to 0.0390625
- grad_out: bfloat16 [512, 12288], P(('gx', 'gy'), 'gz'), may hold values from -6 to 6
Outputs:
- output: bfloat16 [512, 12288], P(('gx', 'gy'), 'gz')
- grad_inputs: bfloat16 [512, 12288], P(('gx', 'gy'), 'gz')
- grad_w_in: bfloat16 [12288, 24576], P('gz', ('gx', 'gy'))
- grad_w_out: bfloat16 [24576, 12288], P(('gx', 'gy'), 'gz')
The draws below stay inside these ranges and needn't reach their ends.
All inputs are finite; a program needn't handle non-finite values.
Results may differ from the reference program's by a relative error of at most 0.005.
Values may be sent and summed in bfloat16 or wider, within the bound.
No kernel may reach another device: no remote copies, remote signals or barrier semaphores. Data moves between devices by JAX's collectives and lax.ppermute only.
A program may use at most 64 MiB of HBM per device.

```python
import jax
import jax.numpy as jnp
from jax import lax

D = 12288
FF = 24576
TOKENS = 512


def level_of(stream_key, dims, pieces, smallest, high):
    gain = 1.0
    for position, parts in pieces:
        heights = jax.random.uniform(jax.random.fold_in(jax.random.fold_in(stream_key, 6), position), (parts,), jnp.float32, smallest / len(pieces), high / len(pieces))
        gain = gain * jnp.repeat(jnp.exp(heights), dims[position] // parts).reshape((-1,) + (1,) * (len(dims) - 1 - position))
    return gain


def normal_values(rng, shape, spread, bound, pieces=(), dtype=jnp.bfloat16):
    gain = level_of(rng, shape, pieces, -0.22, 0.18) if pieces else 1.0
    array = jax.random.normal(rng, shape, jnp.float32) * spread * gain
    return jnp.minimum(jnp.maximum(array, -bound), bound).astype(dtype)


def setup_inputs(seed: int = 0) -> dict:
    keys = jax.random.split(jax.random.key(seed), 5)
    return {
        "inputs": normal_values(keys[0], (TOKENS, D), 1.0, 6.0, ((0, 32), (1, 8))),
        "w_in": normal_values(keys[1], (D, FF), D ** -0.5, 0.0546875, ((0, 8), (1, 32))),
        "w_out": normal_values(keys[2], (FF, D), FF ** -0.5, 0.0390625, ((0, 32), (1, 8))),
        "grad_out": normal_values(keys[3], (TOKENS, D), 1.0, 6.0, ((0, 32), (1, 8))),
    }


gelu_scale = 0.7978845608028654
cubic_term = 0.044715


def gelu_parts(value):
    inner = gelu_scale * (value + cubic_term * value * value * value)
    tanh_part = jnp.tanh(inner)
    result = 0.5 * value * (1.0 + tanh_part)
    slope = 0.5 * (1.0 + tanh_part) + 0.5 * value * (1.0 - tanh_part * tanh_part) * gelu_scale * (1.0 + 3.0 * cubic_term * value * value)
    return result, slope


def reference(inputs, w_in, w_out, grad_out):
    preact = jnp.dot(inputs, w_in, preferred_element_type=jnp.float32)
    result, slope = gelu_parts(preact)
    hidden = result.astype(jnp.bfloat16)
    output = jnp.dot(hidden, w_out, preferred_element_type=jnp.float32).astype(jnp.bfloat16)
    grad_hidden = lax.dot_general(grad_out, w_out, (((1,), (1,)), ((), ())), preferred_element_type=jnp.float32)
    grad_pre = (grad_hidden * slope).astype(jnp.bfloat16)
    grad_inputs = lax.dot_general(grad_pre, w_in, (((1,), (1,)), ((), ())), preferred_element_type=jnp.float32).astype(jnp.bfloat16)
    grad_w_in = lax.dot_general(inputs, grad_pre, (((0,), (0,)), ((), ())), preferred_element_type=jnp.float32).astype(jnp.bfloat16)
    grad_w_out = lax.dot_general(hidden, grad_out, (((0,), (0,)), ((), ())), preferred_element_type=jnp.float32).astype(jnp.bfloat16)
    return output, grad_inputs, grad_w_in, grad_w_out
```

```python
import functools

import jax
import jax.numpy as jnp
from jax import lax
from jax.experimental import pallas as pl
from jax.experimental.pallas import tpu as pltpu
from jax.sharding import PartitionSpec as P

gelu_scale = 0.7978845608028654
cubic_term = 0.044715
tile = 256
bf16 = jnp.bfloat16
f32 = jnp.float32


def gelu_parts(value):
    inner = gelu_scale * (value + cubic_term * value * value * value)
    tanh_part = jnp.tanh(inner)
    result = 0.5 * value * (1.0 + tanh_part)
    slope = 0.5 * (1.0 + tanh_part) + 0.5 * value * (1.0 - tanh_part * tanh_part) * gelu_scale * (
        1.0 + 3.0 * cubic_term * value * value
    )
    return (result, slope)


def plane_peer(index, dx, dz):
    return ((index // 2 + dx) % 4) * 2 + (index % 2 + dz) % 2


plane_steps = [(dx, dz) for dx in range(4) for dz in range(2)]


def from_axis(value, axis, size, step):
    return lax.ppermute(value, axis, [((i + step) % size, i) for i in range(size)])


def to_axis(value, axis, size, step):
    return lax.ppermute(value, axis, [(i, (i + step) % size) for i in range(size)])


def other_core(value):
    return lax.ppermute(value, "gy", [(i, i ^ 1) for i in range(8)])


def from_plane(value, step):
    return lax.ppermute(value, "gz", [(plane_peer(i, *step), i) for i in range(8)])


def to_plane(value, step):
    return lax.ppermute(value, "gz", [(i, plane_peer(i, *step)) for i in range(8)])


def product(left, right, transposed):
    dims = (((1,), (1,)), ((), ())) if transposed else (((1,), (0,)), ((), ()))
    return lax.dot_general(left, right, dims, preferred_element_type=f32)


def columns_of(weight_ref, start, transposed):
    if transposed:
        return weight_ref[pl.ds(start, tile), :]
    return weight_ref[:, pl.ds(start, tile)]


def width_kernel(transposed, index_ref, *refs):
    pieces, weight_ref = refs[:8], refs[8]
    whole_ref, own_ref, sends, acc = refs[9], refs[10], refs[11:18], refs[18]
    me = index_ref[0]
    for i, piece in enumerate(pieces):
        whole_ref[64 * i : 64 * (i + 1), :] = piece[...]

    @pl.loop(0, own_ref.shape[1] // tile)
    def _(j):
        start = pl.multiple_of(j * tile, tile)
        acc[...] = product(whole_ref[...], columns_of(weight_ref, start, transposed), transposed)
        own_ref[:, pl.ds(start, tile)] = acc[pl.ds(pl.multiple_of(me * 64, 64), 64), :]
        for step, send in zip(plane_steps[1:], sends):
            row = pl.multiple_of(plane_peer(me, *step) * 64, 64)
            send[:, pl.ds(start, tile)] = acc[pl.ds(row, 64), :].astype(bf16)


def width_product(index, pieces, weight, transposed):
    width = pieces[0].shape[1]
    units = weight.shape[0] if transposed else weight.shape[1]
    vmem = pl.BlockSpec(memory_space=pltpu.VMEM)
    outs = pl.pallas_call(
        functools.partial(width_kernel, transposed),
        out_shape=[
            jax.ShapeDtypeStruct((512, width), bf16),
            jax.ShapeDtypeStruct((64, units), f32),
        ]
        + [jax.ShapeDtypeStruct((64, units), bf16)] * 7,
        in_specs=[pl.BlockSpec(memory_space=pltpu.SMEM)] + [vmem] * 9,
        out_specs=[vmem] * 9,
        scratch_shapes=[pltpu.VMEM((512, tile), f32)],
        compiler_params=pltpu.CompilerParams(vmem_limit_bytes=24 * 2**20),
        cost_estimate=pl.CostEstimate(
            flops=2 * 512 * width * units, bytes_accessed=6 * 2**20, transcendentals=0
        ),
        name="width_product",
    )(index, *pieces, weight)
    return outs[0], outs[1], outs[2:]


def units_kernel(transposed, index_ref, *refs):
    pieces, weight_ref, whole_ref, far_ref = refs[:8], refs[8], refs[9], refs[10]
    me = index_ref[0]
    for step, piece in zip(plane_steps, pieces):
        row = pl.multiple_of(plane_peer(me, *step) * 64, 64)
        whole_ref[pl.ds(row, 64), :] = piece[...]

    @pl.loop(0, far_ref.shape[1] // tile)
    def _(j):
        start = pl.multiple_of(j * tile, tile)
        far_ref[:, pl.ds(start, tile)] = product(
            whole_ref[256:, :], columns_of(weight_ref, start, transposed), transposed
        )


def near_kernel(transposed, whole_ref, weight_ref, near_ref):
    @pl.loop(0, near_ref.shape[1] // tile)
    def _(j):
        start = pl.multiple_of(j * tile, tile)
        near_ref[:, pl.ds(start, tile)] = product(
            whole_ref[:256, :], columns_of(weight_ref, start, transposed), transposed
        )


def units_product(index, pieces, weight, transposed):
    units = pieces[0].shape[1]
    width = weight.shape[0] if transposed else weight.shape[1]
    vmem = pl.BlockSpec(memory_space=pltpu.VMEM)
    cost = pl.CostEstimate(
        flops=2 * 256 * width * units, bytes_accessed=5 * 2**20, transcendentals=0
    )
    whole, far = pl.pallas_call(
        functools.partial(units_kernel, transposed),
        out_shape=[
            jax.ShapeDtypeStruct((512, units), bf16),
            jax.ShapeDtypeStruct((256, width), f32),
        ],
        in_specs=[pl.BlockSpec(memory_space=pltpu.SMEM)] + [vmem] * 9,
        out_specs=[vmem] * 2,
        compiler_params=pltpu.CompilerParams(vmem_limit_bytes=24 * 2**20),
        cost_estimate=cost,
        name="units_product",
    )(index, *pieces, weight)
    far = other_core(far)
    near = pl.pallas_call(
        functools.partial(near_kernel, transposed),
        out_shape=jax.ShapeDtypeStruct((256, width), f32),
        in_specs=[vmem] * 2,
        out_specs=vmem,
        compiler_params=pltpu.CompilerParams(vmem_limit_bytes=24 * 2**20),
        cost_estimate=cost,
        name="near_product",
    )(whole, weight)
    return whole, near, far


def gather_tokens(shard):
    column = jnp.concatenate([shard] + [from_axis(shard, "gx", 4, d) for d in (1, 2, 3)], axis=0)
    pieces = [column] + [from_axis(column, "gy", 8, 2 * d) for d in (1, 2, 3)]
    return pieces + [other_core(piece) for piece in pieces]


def scatter_tokens(near, far):
    total = near + far
    mine = total[:64]
    parts = [to_axis(total[64 * d : 64 * (d + 1)].astype(bf16), "gy", 8, 2 * d) for d in (1, 2, 3)]
    column = mine + sum(part.astype(f32) for part in parts)
    ends = [to_axis(column[16 * d : 16 * (d + 1)], "gx", 4, d) for d in (1, 2, 3)]
    return (column[:16] + sum(ends)).astype(bf16)


def on_device(inputs, w_in, w_out, grad_out):
    index = jnp.reshape(lax.axis_index("gz"), (1,)).astype(jnp.int32)
    input_pieces = gather_tokens(inputs)
    grad_pieces = gather_tokens(grad_out)
    all_inputs, preact, sends = width_product(index, input_pieces, w_in, False)
    for step, send in zip(plane_steps[1:], sends):
        preact = preact + to_plane(send, step).astype(f32)
    result, slope = gelu_parts(preact)
    hidden = result.astype(bf16)
    hidden_pieces = [hidden] + [from_plane(hidden, step) for step in plane_steps[1:]]
    all_grads, grad_hidden, sends = width_product(index, grad_pieces, w_out, True)
    for step, send in zip(plane_steps[1:], sends):
        grad_hidden = grad_hidden + to_plane(send, step).astype(f32)
    grad_pre = (grad_hidden * slope).astype(bf16)
    grad_pre_pieces = [grad_pre] + [from_plane(grad_pre, step) for step in plane_steps[1:]]
    hidden_all, near, far = units_product(index, hidden_pieces, w_out, False)
    output = scatter_tokens(near, far)
    grad_pre_all, near, far = units_product(index, grad_pre_pieces, w_in, True)
    grad_inputs = scatter_tokens(near, far)
    grad_w_in = lax.dot_general(
        all_inputs, grad_pre_all, (((0,), (0,)), ((), ())), preferred_element_type=f32
    ).astype(bf16)
    grad_w_out = lax.dot_general(
        hidden_all, all_grads, (((0,), (0,)), ((), ())), preferred_element_type=f32
    ).astype(bf16)
    return (output, grad_inputs, grad_w_in, grad_w_out)


def solution(mesh):
    in_specs = (
        P(("gx", "gy"), "gz"),
        P("gz", ("gx", "gy")),
        P(("gx", "gy"), "gz"),
        P(("gx", "gy"), "gz"),
    )
    out_specs = (
        P(("gx", "gy"), "gz"),
        P(("gx", "gy"), "gz"),
        P("gz", ("gx", "gy")),
        P(("gx", "gy"), "gz"),
    )
    return jax.shard_map(
        on_device, mesh=mesh, in_specs=in_specs, out_specs=out_specs, check_vma=False
    )
```

```python
import functools

import jax
import jax.numpy as jnp
from jax import lax
from jax.experimental import pallas as pl
from jax.experimental.pallas import tpu as pltpu
from jax.sharding import PartitionSpec as P

gelu_scale = 0.7978845608028654
cubic_term = 0.044715
tile = 256
bf16 = jnp.bfloat16
f32 = jnp.float32
same_core = [[2 * y + c for y in range(4)] for c in range(2)]


def gelu_parts(value):
    inner = gelu_scale * (value + cubic_term * value * value * value)
    tanh_part = jnp.tanh(inner)
    result = 0.5 * value * (1.0 + tanh_part)
    slope = 0.5 * (1.0 + tanh_part) + 0.5 * value * (1.0 - tanh_part * tanh_part) * gelu_scale * (
        1.0 + 3.0 * cubic_term * value * value
    )
    return (result, slope)


def from_gx(value, step):
    return lax.ppermute(value, "gx", [((i + step) % 4, i) for i in range(4)])


def to_gx(value, step):
    return lax.ppermute(value, "gx", [(i, (i + step) % 4) for i in range(4)])


def other_core(value):
    return lax.ppermute(value, "gy", [(i, i ^ 1) for i in range(8)])


def over_y(value):
    return lax.all_to_all(value, "gy", 0, 0, tiled=True, axis_index_groups=same_core)


def over_gz(value):
    return lax.all_to_all(value, "gz", 0, 0, tiled=True)


def product(left, right, transposed):
    dims = (((1,), (1,)), ((), ())) if transposed else (((1,), (0,)), ((), ()))
    return lax.dot_general(left, right, dims, preferred_element_type=f32)


def columns_of(weight_ref, start, transposed):
    if transposed:
        return weight_ref[pl.ds(start, tile), :]
    return weight_ref[:, pl.ds(start, tile)]


def call(kernel, name, outs, args, scratch=(), flops=0, moved=0, scalars=1):
    vmem = pl.BlockSpec(memory_space=pltpu.VMEM)
    return pl.pallas_call(
        kernel,
        out_shape=[jax.ShapeDtypeStruct(*out) for out in outs],
        in_specs=[pl.BlockSpec(memory_space=pltpu.SMEM)] * scalars + [vmem] * (len(args) - scalars),
        out_specs=[vmem] * len(outs),
        scratch_shapes=[pltpu.VMEM(*shape) for shape in scratch],
        compiler_params=pltpu.CompilerParams(vmem_limit_bytes=16 * 2**20),
        cost_estimate=pl.CostEstimate(flops=flops, bytes_accessed=moved, transcendentals=0),
        name=name,
    )(*args)


def column_gather_kernel(inputs_ref, grads_ref, *refs):
    out_ref = refs[3]
    for y in range(4):
        out_ref[y, 0:16, :] = inputs_ref[...]
        out_ref[y, 64:80, :] = grads_ref[...]
        for step in (1, 2, 3):
            out_ref[y, 16 * step : 16 * step + 16, :] = refs[step - 1][0:16, :]
            out_ref[y, 64 + 16 * step : 80 + 16 * step, :] = refs[step - 1][16:32, :]


def width_kernel(
    index_ref, near_ref, far_ref, w_in_ref, w_out_ref,
    inputs_ref, grads_ref, own_ref, send_ref, acc,
):
    me = index_ref[0]
    for part, whole in ((0, inputs_ref), (1, grads_ref)):
        for half, source in ((0, near_ref), (1, far_ref)):
            for y in range(4):
                row = 256 * half + 64 * y
                whole[row : row + 64, :] = source[y, 64 * part : 64 * part + 64, :]

    @pl.loop(0, own_ref.shape[1] // tile)
    def _(j):
        start = pl.multiple_of(j * tile, tile)
        for part, whole, weight, transposed in (
            (0, inputs_ref, w_in_ref, False),
            (1, grads_ref, w_out_ref, True),
        ):
            rows = slice(64 * part, 64 * part + 64)
            acc[part] = product(whole[...], columns_of(weight, start, transposed), transposed)
            own_ref[rows, pl.ds(start, tile)] = acc[part, pl.ds(pl.multiple_of(me * 64, 64), 64), :]
            for peer in range(8):
                send_ref[peer, rows, pl.ds(start, tile)] = acc[
                    part, 64 * peer : 64 * peer + 64, :
                ].astype(bf16)


def activation_kernel(index_ref, parts_ref, own_ref, out_ref):
    me = index_ref[0]

    @pl.loop(0, 4)
    def _(j):
        sums = []
        for part in range(2):
            rows = pl.ds(pl.multiple_of(64 * part + j * 16, 16), 16)
            total = own_ref[rows, :]
            for peer in range(8):
                total = total + jnp.where(peer == me, 0.0, parts_ref[peer, rows, :].astype(f32))
            sums.append(total)
        result, slope = gelu_parts(sums[0])
        for part, value in ((0, result), (1, sums[1] * slope)):
            rows = pl.ds(pl.multiple_of(64 * part + j * 16, 16), 16)
            rounded = value.astype(bf16)
            for peer in range(8):
                out_ref[peer, rows, :] = rounded


def far_kernel(part, transposed, parts_ref, weight_ref, whole_ref, far_ref):
    for share in range(8):
        whole_ref[64 * share : 64 * share + 64, :] = parts_ref[share, 64 * part : 64 * part + 64, :]

    @pl.loop(0, far_ref.shape[1] // tile)
    def _(j):
        start = pl.multiple_of(j * tile, tile)
        far_ref[:, pl.ds(start, tile)] = product(
            whole_ref[256:, :], columns_of(weight_ref, start, transposed), transposed
        )


def near_kernel(
    index_ref, hidden_ref, grad_pre_ref, w_out_ref, w_in_ref, far_hidden_ref, far_grad_ref,
    own_ref, send_ref, acc,
):
    me = lax.shift_right_logical(index_ref[0], 1)

    @pl.loop(0, own_ref.shape[1] // tile)
    def _(j):
        start = pl.multiple_of(j * tile, tile)
        cols = pl.ds(start, tile)
        for part, whole, weight, far, transposed in (
            (0, hidden_ref, w_out_ref, far_hidden_ref, False),
            (1, grad_pre_ref, w_in_ref, far_grad_ref, True),
        ):
            rows = slice(64 * part, 64 * part + 64)
            acc[part] = far[:, cols] + product(
                whole[:256, :], columns_of(weight, start, transposed), transposed
            )
            own_ref[rows, cols] = acc[part, pl.ds(pl.multiple_of(me * 64, 64), 64), :]
            for peer in range(4):
                send_ref[peer, rows, cols] = acc[part, 64 * peer : 64 * peer + 64, :].astype(bf16)


def column_kernel(index_ref, parts_ref, own_ref, mine_ref, *sends):
    me = lax.shift_right_logical(index_ref[0], 1)
    for step in range(4):
        for part in range(2):
            rows = slice(64 * part + 16 * step, 64 * part + 16 * step + 16)
            total = own_ref[rows, :]
            for peer in range(4):
                total = total + jnp.where(peer == me, 0.0, parts_ref[peer, rows, :].astype(f32))
            if step == 0:
                mine_ref[16 * part : 16 * part + 16, :] = total
            else:
                sends[step - 1][16 * part : 16 * part + 16, :] = total.astype(bf16)


def on_device(inputs, w_in, w_out, grad_out):
    width, units = w_in.shape
    gz_index = jnp.reshape(lax.axis_index("gz"), (1,)).astype(jnp.int32)
    y_index = jnp.reshape(lax.axis_index("gy"), (1,)).astype(jnp.int32)
    both = jnp.concatenate([inputs, grad_out], axis=0)
    (column,) = call(
        column_gather_kernel,
        "column_gather",
        [((4, 128, width), bf16)],
        [inputs, grad_out] + [from_gx(both, step) for step in (1, 2, 3)],
        moved=2 * 2**20,
        scalars=0,
    )
    near = over_y(column)
    far = other_core(near)
    all_inputs, all_grads, own, sends = call(
        width_kernel,
        "width_product",
        [
            ((512, width), bf16),
            ((512, width), bf16),
            ((128, units), f32),
            ((8, 128, units), bf16),
        ],
        [gz_index, near, far, w_in, w_out],
        scratch=[((2, 512, tile), f32)],
        flops=4 * 512 * width * units,
        moved=12 * 2**20,
    )
    (shares,) = call(
        activation_kernel,
        "activation",
        [((8, 128, units), bf16)],
        [gz_index, over_gz(sends), own],
        moved=4 * 2**20,
    )
    gathered = over_gz(shares)
    far_flops = 2 * 256 * width * units
    hidden_all, far_hidden = call(
        functools.partial(far_kernel, 0, False),
        "far_hidden",
        [((512, units), bf16), ((256, width), f32)],
        [gathered, w_out],
        flops=far_flops,
        moved=6 * 2**20,
        scalars=0,
    )
    grad_pre_all, far_grad = call(
        functools.partial(far_kernel, 1, True),
        "far_grad",
        [((512, units), bf16), ((256, width), f32)],
        [gathered, w_in],
        flops=far_flops,
        moved=6 * 2**20,
        scalars=0,
    )
    own, sends = call(
        near_kernel,
        "near_product",
        [((128, width), f32), ((4, 128, width), bf16)],
        [y_index, hidden_all, grad_pre_all, w_out, w_in, other_core(far_hidden), other_core(far_grad)],
        scratch=[((2, 256, tile), f32)],
        flops=2 * far_flops,
        moved=12 * 2**20,
    )
    mine, *sends = call(
        column_kernel,
        "column_sum",
        [((32, width), f32)] + [((32, width), bf16)] * 3,
        [y_index, over_y(sends), own],
        moved=4 * 2**20,
    )
    ends = [to_gx(send, step) for step, send in zip((1, 2, 3), sends)]
    result = (mine + sum(end.astype(f32) for end in ends)).astype(bf16)
    grad_w_in = lax.dot_general(
        all_inputs, grad_pre_all, (((0,), (0,)), ((), ())), preferred_element_type=f32
    ).astype(bf16)
    grad_w_out = lax.dot_general(
        hidden_all, all_grads, (((0,), (0,)), ((), ())), preferred_element_type=f32
    ).astype(bf16)
    return (result[:16], result[16:], grad_w_in, grad_w_out)


def solution(mesh):
    in_specs = (
        P(("gx", "gy"), "gz"),
        P("gz", ("gx", "gy")),
        P(("gx", "gy"), "gz"),
        P(("gx", "gy"), "gz"),
    )
    out_specs = (
        P(("gx", "gy"), "gz"),
        P(("gx", "gy"), "gz"),
        P("gz", ("gx", "gy")),
        P(("gx", "gy"), "gz"),
    )
    return jax.shard_map(
        on_device, mesh=mesh, in_specs=in_specs, out_specs=out_specs, check_vma=False
    )
```

```python
import functools

import jax
import jax.numpy as jnp
from jax import lax
from jax.experimental import pallas as pl
from jax.experimental.pallas import tpu as pltpu
from jax.sharding import PartitionSpec as P

gelu_scale = 0.7978845608028654
cubic_term = 0.044715
tile = 256
bf16 = jnp.bfloat16
f32 = jnp.float32


def gelu_parts(value):
    inner = gelu_scale * (value + cubic_term * value * value * value)
    tanh_part = jnp.tanh(inner)
    result = 0.5 * value * (1.0 + tanh_part)
    slope = 0.5 * (1.0 + tanh_part) + 0.5 * value * (1.0 - tanh_part * tanh_part) * gelu_scale * (
        1.0 + 3.0 * cubic_term * value * value
    )
    return (result, slope)


def from_gx(value, step):
    return lax.ppermute(value, "gx", [((i + step) % 4, i) for i in range(4)])


def to_gx(value, step):
    return lax.ppermute(value, "gx", [(i, (i + step) % 4) for i in range(4)])


def other_core(value):
    return lax.ppermute(value, "gy", [(i, i ^ 1) for i in range(8)])


def from_y(value, step):
    return lax.ppermute(value, "gy", [((i + 2 * step) % 8, i) for i in range(8)])


def to_y(value, step):
    return lax.ppermute(value, "gy", [(i, (i + 2 * step) % 8) for i in range(8)])


def over_gz(value):
    return lax.all_to_all(value, "gz", 0, 0, tiled=True)


def product(left, right, transposed):
    dims = (((1,), (1,)), ((), ())) if transposed else (((1,), (0,)), ((), ()))
    return lax.dot_general(left, right, dims, preferred_element_type=f32)


def columns_of(weight_ref, start, transposed):
    if transposed:
        return weight_ref[pl.ds(start, tile), :]
    return weight_ref[:, pl.ds(start, tile)]


def call(kernel, name, outs, args, scratch=(), flops=0, moved=0, scalars=0, aliases=None):
    vmem = pl.BlockSpec(memory_space=pltpu.VMEM)
    return pl.pallas_call(
        kernel,
        out_shape=[jax.ShapeDtypeStruct(*out) for out in outs],
        in_specs=[pl.BlockSpec(memory_space=pltpu.SMEM)] * scalars + [vmem] * (len(args) - scalars),
        out_specs=[vmem] * len(outs),
        scratch_shapes=[pltpu.VMEM(*shape) for shape in scratch],
        input_output_aliases=aliases or {},
        compiler_params=pltpu.CompilerParams(vmem_limit_bytes=8 * 2**20),
        cost_estimate=pl.CostEstimate(flops=flops, bytes_accessed=moved, transcendentals=0),
        name=name,
    )(*args)


def stack_kernel(*refs):
    rows = refs[0].shape[0]
    for i, piece in enumerate(refs[:4]):
        refs[4][rows * i : rows * (i + 1), :] = piece[...]


def stack(pieces, name):
    rows, width = pieces[0].shape
    return call(stack_kernel, name, [((4 * rows, width), bf16)], pieces, moved=2**20)[0]


def width_kernel(part, transposed, index_ref, near_ref, far_ref, weight_ref, *refs):
    whole_ref, own_ref, send_ref, acc = refs[-4:]
    me = index_ref[0]
    rows = slice(64 * part, 64 * part + 64)
    whole_ref[:256, :] = near_ref[...]
    whole_ref[256:, :] = far_ref[...]

    @pl.loop(0, own_ref.shape[1] // tile)
    def _(j):
        start = pl.multiple_of(j * tile, tile)
        cols = pl.ds(start, tile)
        acc[...] = product(whole_ref[...], columns_of(weight_ref, start, transposed), transposed)
        own_ref[:, cols] = acc[pl.ds(pl.multiple_of(me * 64, 64), 64), :]
        for peer in range(8):
            send_ref[peer, rows, cols] = acc[64 * peer : 64 * peer + 64, :].astype(bf16)


def width_product(part, index, near, far, weight, sends):
    width = near.shape[1]
    units = weight.shape[0] if part else weight.shape[1]
    return call(
        functools.partial(width_kernel, part, bool(part)),
        "width_grad" if part else "width_inputs",
        [((512, width), bf16), ((64, units), f32), ((8, 128, units), bf16)],
        [index, near, far, weight] + sends,
        scratch=[((512, tile), f32)],
        flops=2 * 512 * width * units,
        moved=6 * 2**20,
        scalars=1,
        aliases={4: 2} if sends else None,
    )


def activation_kernel(index_ref, parts_ref, preact_ref, grad_ref, out_ref):
    me = index_ref[0]

    @pl.loop(0, 4)
    def _(j):
        sums = []
        for part, own_ref in ((0, preact_ref), (1, grad_ref)):
            total = own_ref[pl.ds(pl.multiple_of(j * 16, 16), 16), :]
            rows = pl.ds(pl.multiple_of(64 * part + j * 16, 16), 16)
            for peer in range(8):
                total = total + jnp.where(peer == me, 0.0, parts_ref[peer, rows, :].astype(f32))
            sums.append(total)
        result, slope = gelu_parts(sums[0])
        for part, value in ((0, result), (1, sums[1] * slope)):
            rows = pl.ds(pl.multiple_of(64 * part + j * 16, 16), 16)
            rounded = value.astype(bf16)
            for peer in range(8):
                out_ref[peer, rows, :] = rounded


def far_kernel(part, transposed, parts_ref, weight_ref, whole_ref, far_ref):
    for share in range(8):
        whole_ref[64 * share : 64 * share + 64, :] = parts_ref[share, 64 * part : 64 * part + 64, :]

    @pl.loop(0, far_ref.shape[1] // tile)
    def _(j):
        start = pl.multiple_of(j * tile, tile)
        far_ref[:, pl.ds(start, tile)] = product(
            whole_ref[256:, :], columns_of(weight_ref, start, transposed), transposed
        )


def near_kernel(transposed, whole_ref, weight_ref, far_ref, mine_ref, *refs):
    sends, acc = refs[:3], refs[3]

    @pl.loop(0, mine_ref.shape[1] // tile)
    def _(j):
        start = pl.multiple_of(j * tile, tile)
        cols = pl.ds(start, tile)
        acc[...] = far_ref[:, cols] + product(
            whole_ref[:256, :], columns_of(weight_ref, start, transposed), transposed
        )
        mine_ref[:, cols] = acc[:64, :]
        for step in (1, 2, 3):
            sends[step - 1][:, cols] = acc[64 * step : 64 * step + 64, :].astype(bf16)


def column_kernel(own_ref, first_ref, second_ref, third_ref, mine_ref, *sends):
    for step in range(4):
        rows = slice(16 * step, 16 * step + 16)
        total = own_ref[rows, :]
        for part in (first_ref, second_ref, third_ref):
            total = total + part[rows, :].astype(f32)
        if step == 0:
            mine_ref[...] = total
        else:
            sends[step - 1][...] = total.astype(bf16)


def last_kernel(own_ref, first_ref, second_ref, third_ref, out_ref):
    total = own_ref[...]
    for part in (first_ref, second_ref, third_ref):
        total = total + part[...].astype(f32)
    out_ref[...] = total.astype(bf16)


def units_far(part, gathered, weight):
    units = gathered.shape[2]
    width = weight.shape[0] if part else weight.shape[1]
    whole, far = call(
        functools.partial(far_kernel, part, bool(part)),
        "far_grad" if part else "far_hidden",
        [((512, units), bf16), ((256, width), f32)],
        [gathered, weight],
        flops=2 * 256 * width * units,
        moved=6 * 2**20,
    )
    return whole, other_core(far)


def units_near(part, whole, weight, far):
    units, width = whole.shape[1], far.shape[1]
    mine, *sends = call(
        functools.partial(near_kernel, bool(part)),
        "near_grad" if part else "near_hidden",
        [((64, width), f32)] + [((64, width), bf16)] * 3,
        [whole, weight, far],
        scratch=[((256, tile), f32)],
        flops=2 * 256 * width * units,
        moved=6 * 2**20,
    )
    return mine, [to_y(send, step) for step, send in zip((1, 2, 3), sends)]


def column_sum(mine, parts):
    width = mine.shape[1]
    mine, *sends = call(
        column_kernel,
        "column_sum",
        [((16, width), f32)] + [((16, width), bf16)] * 3,
        [mine] + parts,
        moved=2**20,
    )
    return mine, [to_gx(send, step) for step, send in zip((1, 2, 3), sends)]


def last_sum(mine, parts):
    return call(last_kernel, "last_sum", [(mine.shape, bf16)], [mine] + parts, moved=2**18)[0]


def on_device(inputs, w_in, w_out, grad_out):
    width, units = w_in.shape
    index = jnp.reshape(lax.axis_index("gz"), (1,)).astype(jnp.int32)
    steps = (1, 2, 3)
    columns = [[shard] + [from_gx(shard, step) for step in steps] for shard in (inputs, grad_out)]
    columns = [stack(column, "column") for column in columns]
    planes = [[column] + [from_y(column, step) for step in steps] for column in columns]
    near = stack(planes[0], "plane")
    all_inputs, preact, sends = width_product(0, index, near, other_core(near), w_in, [])
    plane, sends = lax.optimization_barrier((planes[1], sends))
    near = stack(plane, "plane")
    all_grads, grad_hidden, sends = width_product(
        1, index, near, other_core(near), w_out, [sends]
    )
    (shares,) = call(
        activation_kernel,
        "activation",
        [((8, 128, units), bf16)],
        [index, over_gz(sends), preact, grad_hidden],
        moved=4 * 2**20,
        scalars=1,
    )
    gathered = over_gz(shares)
    hidden_all, far_hidden = units_far(0, gathered, w_out)
    grad_pre_all, far_grad = units_far(1, gathered, w_in)
    mine_hidden, parts_hidden = units_near(0, hidden_all, w_out, far_hidden)
    mine_grad, parts_grad = units_near(1, grad_pre_all, w_in, far_grad)
    mine_hidden, parts_hidden = column_sum(mine_hidden, parts_hidden)
    mine_grad, parts_grad = column_sum(mine_grad, parts_grad)
    output = last_sum(mine_hidden, parts_hidden)
    grad_inputs = last_sum(mine_grad, parts_grad)
    grad_w_out = lax.dot_general(
        hidden_all, all_grads, (((0,), (0,)), ((), ())), preferred_element_type=f32
    ).astype(bf16)
    grad_w_in = lax.dot_general(
        all_inputs, grad_pre_all, (((0,), (0,)), ((), ())), preferred_element_type=f32
    ).astype(bf16)
    return (output, grad_inputs, grad_w_in, grad_w_out)


def solution(mesh):
    in_specs = (
        P(("gx", "gy"), "gz"),
        P("gz", ("gx", "gy")),
        P(("gx", "gy"), "gz"),
        P(("gx", "gy"), "gz"),
    )
    out_specs = (
        P(("gx", "gy"), "gz"),
        P(("gx", "gy"), "gz"),
        P("gz", ("gx", "gy")),
        P(("gx", "gy"), "gz"),
    )
    return jax.shard_map(
        on_device, mesh=mesh, in_specs=in_specs, out_specs=out_specs, check_vma=False
    )
```

```python
import functools

import jax
import jax.numpy as jnp
from jax import lax
from jax.experimental import pallas as pl
from jax.experimental.pallas import tpu as pltpu
from jax.sharding import PartitionSpec as P

gelu_scale = 0.7978845608028654
cubic_term = 0.044715
tile = 256
bf16 = jnp.bfloat16
f32 = jnp.float32


def gelu_parts(value):
    inner = gelu_scale * (value + cubic_term * value * value * value)
    tanh_part = jnp.tanh(inner)
    result = 0.5 * value * (1.0 + tanh_part)
    slope = 0.5 * (1.0 + tanh_part) + 0.5 * value * (1.0 - tanh_part * tanh_part) * gelu_scale * (
        1.0 + 3.0 * cubic_term * value * value
    )
    return (result, slope)


def from_gx(value, step):
    return lax.ppermute(value, "gx", [((i + step) % 4, i) for i in range(4)])


def to_gx(value, step):
    return lax.ppermute(value, "gx", [(i, (i + step) % 4) for i in range(4)])


def other_core(value):
    return lax.ppermute(value, "gy", [(i, i ^ 1) for i in range(8)])


def from_y(value, step):
    return lax.ppermute(value, "gy", [((i + 2 * step) % 8, i) for i in range(8)])


def to_y(value, step):
    return lax.ppermute(value, "gy", [(i, (i + 2 * step) % 8) for i in range(8)])


def over_gz(value):
    return lax.all_to_all(value, "gz", 0, 0, tiled=True)


def product(left, right, transposed):
    dims = (((1,), (1,)), ((), ())) if transposed else (((1,), (0,)), ((), ()))
    return lax.dot_general(left, right, dims, preferred_element_type=f32)


def columns_of(weight_ref, start, transposed):
    if transposed:
        return weight_ref[pl.ds(start, tile), :]
    return weight_ref[:, pl.ds(start, tile)]


def call(kernel, name, outs, args, scratch=(), flops=0, moved=0, scalars=0, aliases=None):
    vmem = pl.BlockSpec(memory_space=pltpu.VMEM)
    return pl.pallas_call(
        kernel,
        out_shape=[jax.ShapeDtypeStruct(*out) for out in outs],
        in_specs=[pl.BlockSpec(memory_space=pltpu.SMEM)] * scalars + [vmem] * (len(args) - scalars),
        out_specs=[vmem] * len(outs),
        scratch_shapes=[pltpu.VMEM(*shape) for shape in scratch],
        input_output_aliases=aliases or {},
        compiler_params=pltpu.CompilerParams(vmem_limit_bytes=8 * 2**20),
        cost_estimate=pl.CostEstimate(flops=flops, bytes_accessed=moved, transcendentals=0),
        name=name,
    )(*args)


def pair_kernel(inputs_ref, grads_ref, both_ref):
    both_ref[:16, :] = inputs_ref[...]
    both_ref[16:, :] = grads_ref[...]


def columns_kernel(both_ref, first_ref, second_ref, third_ref, inputs_ref, grads_ref):
    for i, source in enumerate((both_ref, first_ref, second_ref, third_ref)):
        inputs_ref[16 * i : 16 * i + 16, :] = source[:16, :]
        grads_ref[16 * i : 16 * i + 16, :] = source[16:, :]


def stack_kernel(*refs):
    rows = refs[0].shape[0]
    for i, piece in enumerate(refs[:4]):
        refs[4][rows * i : rows * (i + 1), :] = piece[...]


def stack(pieces, name):
    rows, width = pieces[0].shape
    return call(stack_kernel, name, [((4 * rows, width), bf16)], pieces, moved=2**20)[0]


def width_kernel(part, transposed, index_ref, near_ref, far_ref, weight_ref, *refs):
    whole_ref, own_ref, send_ref, acc = refs[-4:]
    me = index_ref[0]
    rows = slice(64 * part, 64 * part + 64)
    whole_ref[:256, :] = near_ref[...]
    whole_ref[256:, :] = far_ref[...]

    @pl.loop(0, own_ref.shape[1] // tile)
    def _(j):
        start = pl.multiple_of(j * tile, tile)
        cols = pl.ds(start, tile)
        acc[...] = product(whole_ref[...], columns_of(weight_ref, start, transposed), transposed)
        own_ref[:, cols] = acc[pl.ds(pl.multiple_of(me * 64, 64), 64), :]
        for peer in range(8):
            send_ref[peer, rows, cols] = acc[64 * peer : 64 * peer + 64, :].astype(bf16)


def width_product(part, index, near, far, weight, sends):
    width = near.shape[1]
    units = weight.shape[0] if part else weight.shape[1]
    return call(
        functools.partial(width_kernel, part, bool(part)),
        "width_grad" if part else "width_inputs",
        [((512, width), bf16), ((64, units), f32), ((8, 128, units), bf16)],
        [index, near, far, weight] + sends,
        scratch=[((512, tile), f32)],
        flops=2 * 512 * width * units,
        moved=6 * 2**20,
        scalars=1,
        aliases={4: 2} if sends else None,
    )


def activation_kernel(index_ref, parts_ref, preact_ref, grad_ref, out_ref):
    me = index_ref[0]

    @pl.loop(0, 4)
    def _(j):
        sums = []
        for part, own_ref in ((0, preact_ref), (1, grad_ref)):
            total = own_ref[pl.ds(pl.multiple_of(j * 16, 16), 16), :]
            rows = pl.ds(pl.multiple_of(64 * part + j * 16, 16), 16)
            for peer in range(8):
                total = total + jnp.where(peer == me, 0.0, parts_ref[peer, rows, :].astype(f32))
            sums.append(total)
        result, slope = gelu_parts(sums[0])
        for part, value in ((0, result), (1, sums[1] * slope)):
            rows = pl.ds(pl.multiple_of(64 * part + j * 16, 16), 16)
            rounded = value.astype(bf16)
            for peer in range(8):
                out_ref[peer, rows, :] = rounded


def far_kernel(part, transposed, parts_ref, weight_ref, whole_ref, far_ref):
    for share in range(8):
        whole_ref[64 * share : 64 * share + 64, :] = parts_ref[share, 64 * part : 64 * part + 64, :]

    @pl.loop(0, far_ref.shape[1] // tile)
    def _(j):
        start = pl.multiple_of(j * tile, tile)
        far_ref[:, pl.ds(start, tile)] = product(
            whole_ref[256:, :], columns_of(weight_ref, start, transposed), transposed
        )


def near_kernel(transposed, whole_ref, weight_ref, far_ref, mine_ref, *refs):
    sends, acc = refs[:3], refs[3]

    @pl.loop(0, mine_ref.shape[1] // tile)
    def _(j):
        start = pl.multiple_of(j * tile, tile)
        cols = pl.ds(start, tile)
        acc[...] = far_ref[:, cols] + product(
            whole_ref[:256, :], columns_of(weight_ref, start, transposed), transposed
        )
        mine_ref[:, cols] = acc[:64, :]
        for step in (1, 2, 3):
            sends[step - 1][:, cols] = acc[64 * step : 64 * step + 64, :].astype(bf16)


def column_kernel(*refs):
    mine_ref, sends = refs[8], refs[9:12]
    for step in range(4):
        rows = slice(16 * step, 16 * step + 16)
        for part in range(2):
            total = refs[4 * part][rows, :]
            for piece in refs[4 * part + 1 : 4 * part + 4]:
                total = total + piece[rows, :].astype(f32)
            if step == 0:
                mine_ref[16 * part : 16 * part + 16, :] = total
            else:
                sends[step - 1][16 * part : 16 * part + 16, :] = total.astype(bf16)


def last_kernel(mine_ref, first_ref, second_ref, third_ref, *outs):
    for part, out in enumerate(outs):
        rows = slice(16 * part, 16 * part + 16)
        total = mine_ref[rows, :]
        for piece in (first_ref, second_ref, third_ref):
            total = total + piece[rows, :].astype(f32)
        out[...] = total.astype(bf16)


def units_far(part, gathered, weight):
    units = gathered.shape[2]
    width = weight.shape[0] if part else weight.shape[1]
    whole, far = call(
        functools.partial(far_kernel, part, bool(part)),
        "far_grad" if part else "far_hidden",
        [((512, units), bf16), ((256, width), f32)],
        [gathered, weight],
        flops=2 * 256 * width * units,
        moved=6 * 2**20,
    )
    return whole, other_core(far)


def units_near(part, whole, weight, far):
    units, width = whole.shape[1], far.shape[1]
    mine, *sends = call(
        functools.partial(near_kernel, bool(part)),
        "near_grad" if part else "near_hidden",
        [((64, width), f32)] + [((64, width), bf16)] * 3,
        [whole, weight, far],
        scratch=[((256, tile), f32)],
        flops=2 * 256 * width * units,
        moved=6 * 2**20,
    )
    return mine, [to_y(send, step) for step, send in zip((1, 2, 3), sends)]


def on_device(inputs, w_in, w_out, grad_out):
    width, units = w_in.shape
    index = jnp.reshape(lax.axis_index("gz"), (1,)).astype(jnp.int32)
    steps = (1, 2, 3)
    (both,) = call(pair_kernel, "pair", [((32, width), bf16)], [inputs, grad_out], moved=2**18)
    columns = call(
        columns_kernel,
        "columns",
        [((64, width), bf16)] * 2,
        [both] + [from_gx(both, step) for step in steps],
        moved=2**20,
    )
    planes = [[column] + [from_y(column, step) for step in steps] for column in columns]
    near = stack(planes[0], "plane")
    all_inputs, preact, sends = width_product(0, index, near, other_core(near), w_in, [])
    near = stack(planes[1], "plane")
    all_grads, grad_hidden, sends = width_product(
        1, index, near, other_core(near), w_out, [sends]
    )
    (shares,) = call(
        activation_kernel,
        "activation",
        [((8, 128, units), bf16)],
        [index, over_gz(sends), preact, grad_hidden],
        moved=4 * 2**20,
        scalars=1,
    )
    gathered = over_gz(shares)
    hidden_all, far_hidden = units_far(0, gathered, w_out)
    grad_pre_all, far_grad = units_far(1, gathered, w_in)
    mine_hidden, parts_hidden = units_near(0, hidden_all, w_out, far_hidden)
    mine_grad, parts_grad = units_near(1, grad_pre_all, w_in, far_grad)
    mine, *sends = call(
        column_kernel,
        "column_sums",
        [((32, width), f32)] + [((32, width), bf16)] * 3,
        [mine_hidden] + parts_hidden + [mine_grad] + parts_grad,
        moved=2 * 2**20,
    )
    output, grad_inputs = call(
        last_kernel,
        "last_sums",
        [((16, width), bf16)] * 2,
        [mine] + [to_gx(send, step) for step, send in zip(steps, sends)],
        moved=2**19,
    )
    grad_w_out = lax.dot_general(
        hidden_all, all_grads, (((0,), (0,)), ((), ())), preferred_element_type=f32
    ).astype(bf16)
    grad_w_in = lax.dot_general(
        all_inputs, grad_pre_all, (((0,), (0,)), ((), ())), preferred_element_type=f32
    ).astype(bf16)
    return (output, grad_inputs, grad_w_in, grad_w_out)


def solution(mesh):
    in_specs = (
        P(("gx", "gy"), "gz"),
        P("gz", ("gx", "gy")),
        P(("gx", "gy"), "gz"),
        P(("gx", "gy"), "gz"),
    )
    out_specs = (
        P(("gx", "gy"), "gz"),
        P(("gx", "gy"), "gz"),
        P("gz", ("gx", "gy")),
        P(("gx", "gy"), "gz"),
    )
    return jax.shard_map(
        on_device, mesh=mesh, in_specs=in_specs, out_specs=out_specs, check_vma=False
    )
```

```python
import functools

import jax
import jax.numpy as jnp
from jax import lax
from jax.experimental import pallas as pl
from jax.experimental.pallas import tpu as pltpu
from jax.sharding import PartitionSpec as P

gelu_scale = 0.7978845608028654
cubic_term = 0.044715
tile = 256
bf16 = jnp.bfloat16
f32 = jnp.float32


def gelu_parts(value):
    inner = gelu_scale * (value + cubic_term * value * value * value)
    tanh_part = jnp.tanh(inner)
    result = 0.5 * value * (1.0 + tanh_part)
    slope = 0.5 * (1.0 + tanh_part) + 0.5 * value * (1.0 - tanh_part * tanh_part) * gelu_scale * (
        1.0 + 3.0 * cubic_term * value * value
    )
    return (result, slope)


def from_gx(value, step):
    return lax.ppermute(value, "gx", [((i + step) % 4, i) for i in range(4)])


def to_gx(value, step):
    return lax.ppermute(value, "gx", [(i, (i + step) % 4) for i in range(4)])


def other_core(value):
    return lax.ppermute(value, "gy", [(i, i ^ 1) for i in range(8)])


def from_y(value, step):
    return lax.ppermute(value, "gy", [((i + 2 * step) % 8, i) for i in range(8)])


def to_y(value, step):
    return lax.ppermute(value, "gy", [(i, (i + 2 * step) % 8) for i in range(8)])


def from_x(value, step):
    return lax.ppermute(value, "gz", [((i + 2 * step) % 8, i) for i in range(8)])


def to_x(value, step):
    return lax.ppermute(value, "gz", [(i, (i + 2 * step) % 8) for i in range(8)])


def other_z(value):
    return lax.ppermute(value, "gz", [(i, i ^ 1) for i in range(8)])


def product(left, right, transposed):
    dims = (((1,), (1,)), ((), ())) if transposed else (((1,), (0,)), ((), ()))
    return lax.dot_general(left, right, dims, preferred_element_type=f32)


def columns_of(weight_ref, start, transposed):
    if transposed:
        return weight_ref[pl.ds(start, tile), :]
    return weight_ref[:, pl.ds(start, tile)]


def call(kernel, name, outs, args, scratch=(), flops=0, moved=0, scalars=0, aliases=None):
    vmem = pl.BlockSpec(memory_space=pltpu.VMEM)
    return pl.pallas_call(
        kernel,
        out_shape=[jax.ShapeDtypeStruct(*out) for out in outs],
        in_specs=[pl.BlockSpec(memory_space=pltpu.SMEM)] * scalars + [vmem] * (len(args) - scalars),
        out_specs=[vmem] * len(outs),
        scratch_shapes=[pltpu.VMEM(*shape) for shape in scratch],
        input_output_aliases=aliases or {},
        compiler_params=pltpu.CompilerParams(vmem_limit_bytes=8 * 2**20),
        cost_estimate=pl.CostEstimate(flops=flops, bytes_accessed=moved, transcendentals=0),
        name=name,
    )(*args)


def pair_kernel(inputs_ref, grads_ref, both_ref):
    both_ref[:16, :] = inputs_ref[...]
    both_ref[16:, :] = grads_ref[...]


def columns_kernel(both_ref, first_ref, second_ref, third_ref, inputs_ref, grads_ref):
    for i, source in enumerate((both_ref, first_ref, second_ref, third_ref)):
        inputs_ref[16 * i : 16 * i + 16, :] = source[:16, :]
        grads_ref[16 * i : 16 * i + 16, :] = source[16:, :]


def stack_kernel(*refs):
    rows = refs[0].shape[0]
    for i, piece in enumerate(refs[:4]):
        refs[4][rows * i : rows * (i + 1), :] = piece[...]


def stack(pieces, name):
    rows, width = pieces[0].shape
    return call(stack_kernel, name, [((4 * rows, width), bf16)], pieces, moved=2**20)[0]


def place(index_ref):
    me = index_ref[0]
    return lax.shift_right_logical(me, 1), lax.bitwise_and(me, 1)


def block(x, step, size, offset=0):
    return pl.ds(pl.multiple_of(lax.bitwise_and(x + step, 3) * 128 + offset, 64), size)


def width_inputs_kernel(index_ref, near_ref, far_ref, weight_ref, *refs):
    whole_ref, own_ref, sends, acc = refs[0], refs[1], refs[2:5], refs[5]
    x, z = place(index_ref)
    whole_ref[:256, :] = near_ref[...]
    whole_ref[256:, :] = far_ref[...]

    @pl.loop(0, own_ref.shape[1] // tile)
    def _(j):
        start = pl.multiple_of(j * tile, tile)
        cols = pl.ds(start, tile)
        acc[...] = product(whole_ref[...], columns_of(weight_ref, start, False), False)
        own_ref[:, cols] = acc[block(x, 0, 128), :]
        for step in (1, 2, 3):
            sends[step - 1][:, cols] = acc[block(x, step, 128), :].astype(bf16)


def width_grad_kernel(index_ref, near_ref, far_ref, weight_ref, *refs):
    whole_ref, own_ref, send_ref, acc = refs
    x, z = place(index_ref)
    whole_ref[:256, :] = near_ref[...]
    whole_ref[256:, :] = far_ref[...]

    @pl.loop(0, own_ref.shape[1] // tile)
    def _(j):
        start = pl.multiple_of(j * tile, tile)
        cols = pl.ds(start, tile)
        acc[...] = product(whole_ref[...], columns_of(weight_ref, start, True), True)
        for step in range(4):
            rows = slice(64 * step, 64 * step + 64)
            own_ref[rows, cols] = acc[block(x, step, 64, 64 * z), :]
            send_ref[rows, cols] = acc[block(x, step, 64, 64 * (1 - z)), :].astype(bf16)


def sum_x_kernel(index_ref, own_ref, first_ref, second_ref, third_ref, mine_ref, send_ref):
    x, z = place(index_ref)
    for target, half in ((mine_ref, z), (send_ref, 1 - z)):

        @pl.loop(0, 4)
        def _(j):
            rows = pl.ds(pl.multiple_of(64 * half + 16 * j, 16), 16)
            total = own_ref[rows, :]
            for piece in (first_ref, second_ref, third_ref):
                total = total + piece[rows, :].astype(f32)
            target[pl.ds(pl.multiple_of(16 * j, 16), 16), :] = total


def activation_kernel(mine_ref, part_ref, hidden_ref, slope_ref):
    @pl.loop(0, 4)
    def _(j):
        rows = pl.ds(pl.multiple_of(16 * j, 16), 16)
        result, slope = gelu_parts(mine_ref[rows, :] + part_ref[rows, :])
        hidden_ref[rows, :] = result.astype(bf16)
        slope_ref[rows, :] = slope


def sum_z_kernel(own_ref, part_ref, mine_ref, *sends):
    for step in range(4):

        @pl.loop(0, 4)
        def _(j):
            rows = pl.ds(pl.multiple_of(64 * step + 16 * j, 16), 16)
            local = pl.ds(pl.multiple_of(16 * j, 16), 16)
            total = own_ref[rows, :] + part_ref[rows, :].astype(f32)
            if step == 0:
                mine_ref[local, :] = total
            else:
                sends[step - 1][local, :] = total.astype(bf16)


def grad_pre_kernel(mine_ref, first_ref, second_ref, third_ref, slope_ref, out_ref):
    @pl.loop(0, 4)
    def _(j):
        rows = pl.ds(pl.multiple_of(16 * j, 16), 16)
        total = mine_ref[rows, :]
        for piece in (first_ref, second_ref, third_ref):
            total = total + piece[rows, :].astype(f32)
        out_ref[rows, :] = (total * slope_ref[rows, :]).astype(bf16)


def pair_z_kernel(index_ref, own_ref, part_ref, out_ref):
    x, z = place(index_ref)
    out_ref[pl.ds(pl.multiple_of(64 * z, 64), 64), :] = own_ref[...]
    out_ref[pl.ds(pl.multiple_of(64 * (1 - z), 64), 64), :] = part_ref[...]


def far_columns(whole_ref, weight_ref, far_ref, transposed):
    @pl.loop(0, far_ref.shape[1] // tile)
    def _(j):
        start = pl.multiple_of(j * tile, tile)
        far_ref[:, pl.ds(start, tile)] = product(
            whole_ref[256:, :], columns_of(weight_ref, start, transposed), transposed
        )


def far_hidden_kernel(index_ref, *refs):
    pieces, weight_ref, whole_ref, far_ref = refs[:4], refs[4], refs[5], refs[6]
    x, z = place(index_ref)
    for step in range(4):
        whole_ref[block(x, step, 128), :] = pieces[step][...]
    far_columns(whole_ref, weight_ref, far_ref, False)


def far_grad_kernel(index_ref, own_ref, part_ref, weight_ref, whole_ref, far_ref):
    x, z = place(index_ref)
    for step in range(4):
        rows = slice(64 * step, 64 * step + 64)
        whole_ref[block(x, step, 64, 64 * z), :] = own_ref[rows, :]
        whole_ref[block(x, step, 64, 64 * (1 - z)), :] = part_ref[rows, :]
    far_columns(whole_ref, weight_ref, far_ref, True)


def near_kernel(transposed, whole_ref, weight_ref, far_ref, mine_ref, *refs):
    sends, acc = refs[:3], refs[3]

    @pl.loop(0, mine_ref.shape[1] // tile)
    def _(j):
        start = pl.multiple_of(j * tile, tile)
        cols = pl.ds(start, tile)
        acc[...] = far_ref[:, cols] + product(
            whole_ref[:256, :], columns_of(weight_ref, start, transposed), transposed
        )
        mine_ref[:, cols] = acc[:64, :]
        for step in (1, 2, 3):
            sends[step - 1][:, cols] = acc[64 * step : 64 * step + 64, :].astype(bf16)


def column_kernel(*refs):
    mine_ref, sends = refs[8], refs[9:12]
    for step in range(4):
        rows = slice(16 * step, 16 * step + 16)
        for part in range(2):
            total = refs[4 * part][rows, :]
            for piece in refs[4 * part + 1 : 4 * part + 4]:
                total = total + piece[rows, :].astype(f32)
            if step == 0:
                mine_ref[16 * part : 16 * part + 16, :] = total
            else:
                sends[step - 1][16 * part : 16 * part + 16, :] = total.astype(bf16)


def last_kernel(mine_ref, first_ref, second_ref, third_ref, *outs):
    for part, out in enumerate(outs):
        rows = slice(16 * part, 16 * part + 16)
        total = mine_ref[rows, :]
        for piece in (first_ref, second_ref, third_ref):
            total = total + piece[rows, :].astype(f32)
        out[...] = total.astype(bf16)


def units_far(kernel, name, index, pieces, weight, transposed):
    units = pieces[0].shape[1]
    width = weight.shape[0] if transposed else weight.shape[1]
    whole, far = call(
        kernel,
        name,
        [((512, units), bf16), ((256, width), f32)],
        [index] + pieces + [weight],
        flops=2 * 256 * width * units,
        moved=6 * 2**20,
        scalars=1,
    )
    return whole, other_core(far)


def units_near(part, whole, weight, far):
    units, width = whole.shape[1], far.shape[1]
    mine, *sends = call(
        functools.partial(near_kernel, bool(part)),
        "near_grad" if part else "near_hidden",
        [((64, width), f32)] + [((64, width), bf16)] * 3,
        [whole, weight, far],
        scratch=[((256, tile), f32)],
        flops=2 * 256 * width * units,
        moved=6 * 2**20,
    )
    return mine, [to_y(send, step) for step, send in zip((1, 2, 3), sends)]


def on_device(inputs, w_in, w_out, grad_out):
    width, units = w_in.shape
    index = jnp.reshape(lax.axis_index("gz"), (1,)).astype(jnp.int32)
    steps = (1, 2, 3)
    (both,) = call(pair_kernel, "pair", [((32, width), bf16)], [inputs, grad_out], moved=2**18)
    columns = call(
        columns_kernel,
        "columns",
        [((64, width), bf16)] * 2,
        [both] + [from_gx(both, step) for step in steps],
        moved=2**20,
    )
    planes = [[column] + [from_y(column, step) for step in steps] for column in columns]
    near = stack(planes[0], "plane")
    width_flops = 2 * 512 * width * units
    all_inputs, own, *sends = call(
        width_inputs_kernel,
        "width_inputs",
        [((512, width), bf16), ((128, units), f32)] + [((128, units), bf16)] * 3,
        [index, near, other_core(near), w_in],
        scratch=[((512, tile), f32)],
        flops=width_flops,
        moved=6 * 2**20,
        scalars=1,
    )
    mine, send = call(
        sum_x_kernel,
        "sum_x",
        [((64, units), f32)] * 2,
        [index, own] + [to_x(send, step) for step, send in zip(steps, sends)],
        moved=2**20,
        scalars=1,
    )
    hidden, slope = call(
        activation_kernel,
        "activation",
        [((64, units), bf16), ((64, units), f32)],
        [mine, other_z(send)],
        moved=2**20,
    )
    near = stack(planes[1], "plane")
    all_grads, own, send = call(
        width_grad_kernel,
        "width_grad",
        [((512, width), bf16), ((256, units), f32), ((256, units), bf16)],
        [index, near, other_core(near), w_out],
        scratch=[((512, tile), f32)],
        flops=width_flops,
        moved=6 * 2**20,
        scalars=1,
    )
    mine, *sends = call(
        sum_z_kernel,
        "sum_z",
        [((64, units), f32)] + [((64, units), bf16)] * 3,
        [own, other_z(send)],
        moved=2**20,
    )
    (pair,) = call(
        pair_z_kernel,
        "pair_z",
        [((128, units), bf16)],
        [index, hidden, other_z(hidden)],
        moved=2**19,
        scalars=1,
    )
    (grad_pre,) = call(
        grad_pre_kernel,
        "grad_pre",
        [((64, units), bf16)],
        [mine] + [to_x(send, step) for step, send in zip(steps, sends)] + [slope],
        moved=2**20,
    )
    hidden_pieces = [pair] + [from_x(pair, step) for step in steps]
    grad_stack = stack([grad_pre] + [from_x(grad_pre, step) for step in steps], "grad_stack")
    hidden_all, far_hidden = units_far(
        far_hidden_kernel, "far_hidden", index, hidden_pieces, w_out, False
    )
    grad_pre_all, far_grad = units_far(
        far_grad_kernel, "far_grad", index, [grad_stack, other_z(grad_stack)], w_in, True
    )
    mine_hidden, parts_hidden = units_near(0, hidden_all, w_out, far_hidden)
    mine_grad, parts_grad = units_near(1, grad_pre_all, w_in, far_grad)
    mine, *sends = call(
        column_kernel,
        "column_sums",
        [((32, width), f32)] + [((32, width), bf16)] * 3,
        [mine_hidden] + parts_hidden + [mine_grad] + parts_grad,
        moved=2 * 2**20,
    )
    output, grad_inputs = call(
        last_kernel,
        "last_sums",
        [((16, width), bf16)] * 2,
        [mine] + [to_gx(send, step) for step, send in zip(steps, sends)],
        moved=2**19,
    )
    grad_w_out = lax.dot_general(
        hidden_all, all_grads, (((0,), (0,)), ((), ())), preferred_element_type=f32
    ).astype(bf16)
    grad_w_in = lax.dot_general(
        all_inputs, grad_pre_all, (((0,), (0,)), ((), ())), preferred_element_type=f32
    ).astype(bf16)
    return (output, grad_inputs, grad_w_in, grad_w_out)


def solution(mesh):
    in_specs = (
        P(("gx", "gy"), "gz"),
        P("gz", ("gx", "gy")),
        P(("gx", "gy"), "gz"),
        P(("gx", "gy"), "gz"),
    )
    out_specs = (
        P(("gx", "gy"), "gz"),
        P(("gx", "gy"), "gz"),
        P("gz", ("gx", "gy")),
        P(("gx", "gy"), "gz"),
    )
    return jax.shard_map(
        on_device, mesh=mesh, in_specs=in_specs, out_specs=out_specs, check_vma=False
    )
```

```python
import functools

import jax
import jax.numpy as jnp
from jax import lax
from jax.experimental import pallas as pl
from jax.experimental.pallas import tpu as pltpu
from jax.sharding import PartitionSpec as P

gelu_scale = 0.7978845608028654
cubic_term = 0.044715
tile = 256
bf16 = jnp.bfloat16
f32 = jnp.float32


def gelu_parts(value):
    inner = gelu_scale * (value + cubic_term * value * value * value)
    tanh_part = jnp.tanh(inner)
    result = 0.5 * value * (1.0 + tanh_part)
    slope = 0.5 * (1.0 + tanh_part) + 0.5 * value * (1.0 - tanh_part * tanh_part) * gelu_scale * (
        1.0 + 3.0 * cubic_term * value * value
    )
    return (result, slope)


barrier = lax.optimization_barrier


def from_gx(value, step):
    return lax.ppermute(value, "gx", [((i + step) % 4, i) for i in range(4)])


def to_gx(value, step):
    return lax.ppermute(value, "gx", [(i, (i + step) % 4) for i in range(4)])


def other_core(value):
    return lax.ppermute(value, "gy", [(i, i ^ 1) for i in range(8)])


def from_y(value, step):
    return lax.ppermute(value, "gy", [((i + 2 * step) % 8, i) for i in range(8)])


def to_y(value, step):
    return lax.ppermute(value, "gy", [(i, (i + 2 * step) % 8) for i in range(8)])


def from_x(value, step):
    return lax.ppermute(value, "gz", [((i + 2 * step) % 8, i) for i in range(8)])


def to_x(value, step):
    return lax.ppermute(value, "gz", [(i, (i + 2 * step) % 8) for i in range(8)])


def other_z(value):
    return lax.ppermute(value, "gz", [(i, i ^ 1) for i in range(8)])


def product(left, right, transposed):
    dims = (((1,), (1,)), ((), ())) if transposed else (((1,), (0,)), ((), ()))
    return lax.dot_general(left, right, dims, preferred_element_type=f32)


def columns_of(weight_ref, start, transposed):
    if transposed:
        return weight_ref[pl.ds(start, tile), :]
    return weight_ref[:, pl.ds(start, tile)]


def call(kernel, name, outs, args, scratch=(), moved=0, scalars=0, aliases=None):
    vmem = pl.BlockSpec(memory_space=pltpu.VMEM)
    return pl.pallas_call(
        kernel,
        out_shape=[jax.ShapeDtypeStruct(*out) for out in outs],
        in_specs=[pl.BlockSpec(memory_space=pltpu.SMEM)] * scalars + [vmem] * (len(args) - scalars),
        out_specs=[vmem] * len(outs),
        scratch_shapes=[pltpu.VMEM(*shape) for shape in scratch],
        input_output_aliases=aliases or {},
        compiler_params=pltpu.CompilerParams(vmem_limit_bytes=8 * 2**20),
        cost_estimate=pl.CostEstimate(flops=0, bytes_accessed=moved, transcendentals=0),
        name=name,
    )(*args)


def pair_kernel(inputs_ref, grads_ref, both_ref):
    both_ref[:16, :] = inputs_ref[...]
    both_ref[16:, :] = grads_ref[...]


def columns_kernel(both_ref, first_ref, second_ref, third_ref, inputs_ref, grads_ref):
    for i, source in enumerate((both_ref, first_ref, second_ref, third_ref)):
        inputs_ref[16 * i : 16 * i + 16, :] = source[:16, :]
        grads_ref[16 * i : 16 * i + 16, :] = source[16:, :]


def stack_kernel(*refs):
    rows = refs[0].shape[0]
    for i, piece in enumerate(refs[:4]):
        refs[4][rows * i : rows * (i + 1), :] = piece[...]


def stack_two_kernel(*refs):
    for i, piece in enumerate(refs[:4]):
        refs[4 + i // 2][64 * (i % 2) : 64 * (i % 2) + 64, :] = piece[...]


def stack(pieces, name):
    rows, width = pieces[0].shape
    return call(stack_kernel, name, [((4 * rows, width), bf16)], pieces, moved=2**20)[0]


def place(index_ref):
    me = index_ref[0]
    return lax.shift_right_logical(me, 1), lax.bitwise_and(me, 1)


def block(x, step, size, offset=0):
    return pl.ds(pl.multiple_of(lax.bitwise_and(x + step, 3) * 128 + offset, 64), size)


def width_inputs_kernel(index_ref, near_ref, far_ref, weight_ref, *refs):
    whole_ref, own_ref, sends, acc = refs[0], refs[1], refs[2:5], refs[5]
    x, z = place(index_ref)
    whole_ref[:256, :] = near_ref[...]
    whole_ref[256:, :] = far_ref[...]

    @pl.loop(0, own_ref.shape[1] // tile)
    def _(j):
        start = pl.multiple_of(j * tile, tile)
        cols = pl.ds(start, tile)
        acc[...] = product(whole_ref[...], columns_of(weight_ref, start, False), False)
        own_ref[:, cols] = acc[block(x, 0, 128), :]
        for step in (1, 2, 3):
            sends[step - 1][:, cols] = acc[block(x, step, 128), :].astype(bf16)


def width_grad_kernel(index_ref, near_ref, far_ref, weight_ref, *refs):
    whole_ref, own_ref, send_ref, acc = refs
    x, z = place(index_ref)
    whole_ref[:256, :] = near_ref[...]
    whole_ref[256:, :] = far_ref[...]

    @pl.loop(0, own_ref.shape[1] // tile)
    def _(j):
        start = pl.multiple_of(j * tile, tile)
        cols = pl.ds(start, tile)
        acc[...] = product(whole_ref[...], columns_of(weight_ref, start, True), True)
        for step in range(4):
            rows = slice(64 * step, 64 * step + 64)
            own_ref[rows, cols] = acc[block(x, step, 64, 64 * z), :]
            send_ref[rows, cols] = acc[block(x, step, 64, 64 * (1 - z)), :].astype(bf16)


def sum_x_kernel(index_ref, own_ref, first_ref, second_ref, third_ref, mine_ref, send_ref):
    x, z = place(index_ref)
    for target, half in ((mine_ref, z), (send_ref, 1 - z)):

        @pl.loop(0, 4)
        def _(j):
            rows = pl.ds(pl.multiple_of(64 * half + 16 * j, 16), 16)
            total = own_ref[rows, :]
            for piece in (first_ref, second_ref, third_ref):
                total = total + piece[rows, :].astype(f32)
            target[pl.ds(pl.multiple_of(16 * j, 16), 16), :] = total


def activation_kernel(mine_ref, part_ref, hidden_ref, slope_ref):
    @pl.loop(0, 4)
    def _(j):
        rows = pl.ds(pl.multiple_of(16 * j, 16), 16)
        result, slope = gelu_parts(mine_ref[rows, :] + part_ref[rows, :])
        hidden_ref[rows, :] = result.astype(bf16)
        slope_ref[rows, :] = slope


def sum_z_kernel(own_ref, part_ref, mine_ref, *sends):
    for step in range(4):

        @pl.loop(0, 4)
        def _(j):
            rows = pl.ds(pl.multiple_of(64 * step + 16 * j, 16), 16)
            local = pl.ds(pl.multiple_of(16 * j, 16), 16)
            total = own_ref[rows, :] + part_ref[rows, :].astype(f32)
            if step == 0:
                mine_ref[local, :] = total
            else:
                sends[step - 1][local, :] = total.astype(bf16)


def grad_pre_kernel(mine_ref, first_ref, second_ref, third_ref, slope_ref, out_ref):
    @pl.loop(0, 4)
    def _(j):
        rows = pl.ds(pl.multiple_of(16 * j, 16), 16)
        total = mine_ref[rows, :]
        for piece in (first_ref, second_ref, third_ref):
            total = total + piece[rows, :].astype(f32)
        out_ref[rows, :] = (total * slope_ref[rows, :]).astype(bf16)


def pair_z_kernel(index_ref, own_ref, part_ref, out_ref):
    x, z = place(index_ref)
    out_ref[pl.ds(pl.multiple_of(64 * z, 64), 64), :] = own_ref[...]
    out_ref[pl.ds(pl.multiple_of(64 * (1 - z), 64), 64), :] = part_ref[...]


def far_columns(whole_ref, weight_ref, far_ref, transposed):
    @pl.loop(0, far_ref.shape[1] // tile)
    def _(j):
        start = pl.multiple_of(j * tile, tile)
        far_ref[:, pl.ds(start, tile)] = product(
            whole_ref[256:, :], columns_of(weight_ref, start, transposed), transposed
        )


def far_hidden_kernel(index_ref, *refs):
    pieces, weight_ref, whole_ref, far_ref = refs[:4], refs[4], refs[5], refs[6]
    x, z = place(index_ref)
    for step in range(4):
        whole_ref[block(x, step, 128), :] = pieces[step][...]
    far_columns(whole_ref, weight_ref, far_ref, False)


def far_grad_kernel(index_ref, *refs):
    own, parts, weight_ref, whole_ref, far_ref = refs[:2], refs[2:4], refs[4], refs[5], refs[6]
    x, z = place(index_ref)
    for step in range(4):
        rows = slice(64 * (step % 2), 64 * (step % 2) + 64)
        whole_ref[block(x, step, 64, 64 * z), :] = own[step // 2][rows, :]
        whole_ref[block(x, step, 64, 64 * (1 - z)), :] = parts[step // 2][rows, :]
    far_columns(whole_ref, weight_ref, far_ref, True)


def near_kernel(transposed, whole_ref, weight_ref, far_ref, mine_ref, *refs):
    sends, acc = refs[:3], refs[3]

    @pl.loop(0, mine_ref.shape[1] // tile)
    def _(j):
        start = pl.multiple_of(j * tile, tile)
        cols = pl.ds(start, tile)
        acc[...] = far_ref[:, cols] + product(
            whole_ref[:256, :], columns_of(weight_ref, start, transposed), transposed
        )
        mine_ref[:, cols] = acc[:64, :]
        for step in (1, 2, 3):
            sends[step - 1][:, cols] = acc[64 * step : 64 * step + 64, :].astype(bf16)


def column_kernel(*refs):
    mine_ref, sends = refs[8], refs[9:12]
    for step in range(4):
        rows = slice(16 * step, 16 * step + 16)
        for part in range(2):
            total = refs[4 * part][rows, :]
            for piece in refs[4 * part + 1 : 4 * part + 4]:
                total = total + piece[rows, :].astype(f32)
            if step == 0:
                mine_ref[16 * part : 16 * part + 16, :] = total
            else:
                sends[step - 1][16 * part : 16 * part + 16, :] = total.astype(bf16)


def last_kernel(mine_ref, first_ref, second_ref, third_ref, *outs):
    for part, out in enumerate(outs):
        rows = slice(16 * part, 16 * part + 16)
        total = mine_ref[rows, :]
        for piece in (first_ref, second_ref, third_ref):
            total = total + piece[rows, :].astype(f32)
        out[...] = total.astype(bf16)


def units_far(kernel, name, index, pieces, weight, transposed):
    units = pieces[0].shape[1]
    width = weight.shape[0] if transposed else weight.shape[1]
    whole, far = call(
        kernel,
        name,
        [((512, units), bf16), ((256, width), f32)],
        [index] + pieces + [weight],
        moved=6 * 2**20,
        scalars=1,
    )
    return whole, other_core(far)


def units_near(part, whole, weight, far):
    units, width = whole.shape[1], far.shape[1]
    mine, *sends = call(
        functools.partial(near_kernel, bool(part)),
        "near_grad" if part else "near_hidden",
        [((64, width), f32)] + [((64, width), bf16)] * 3,
        [whole, weight, far],
        scratch=[((256, tile), f32)],
        moved=6 * 2**20,
    )
    return mine, [to_y(send, step) for step, send in zip((1, 2, 3), sends)]


def on_device(inputs, w_in, w_out, grad_out):
    width, units = w_in.shape
    index = jnp.reshape(lax.axis_index("gz"), (1,)).astype(jnp.int32)
    steps = (1, 2, 3)
    (both,) = call(pair_kernel, "pair", [((32, width), bf16)], [inputs, grad_out], moved=2**18)
    columns = call(
        columns_kernel,
        "columns",
        [((64, width), bf16)] * 2,
        [both] + [from_gx(both, step) for step in steps],
        moved=2**20,
    )
    planes = [[column] + [from_y(column, step) for step in steps] for column in columns]
    near = stack(planes[0], "plane")
    all_inputs, own, *sends = call(
        width_inputs_kernel,
        "width_inputs",
        [((512, width), bf16), ((128, units), f32)] + [((128, units), bf16)] * 3,
        [index, near, other_core(near), w_in],
        scratch=[((512, tile), f32)],
        moved=6 * 2**20,
        scalars=1,
    )
    parts_inputs, own_inputs = [to_x(send, step) for step, send in zip(steps, sends)], own
    near = stack(planes[1], "plane")
    all_grads, own, send = call(
        width_grad_kernel,
        "width_grad",
        [((512, width), bf16), ((256, units), f32), ((256, units), bf16)],
        [index, near, other_core(near), w_out],
        scratch=[((512, tile), f32)],
        moved=6 * 2**20,
        scalars=1,
    )
    mine_grads, *sends = call(
        sum_z_kernel,
        "sum_z",
        [((64, units), f32)] + [((64, units), bf16)] * 3,
        [own, other_z(send)],
        moved=2**20,
    )
    parts_grads = [to_x(send, step) for step, send in zip(steps, sends)]
    parts_inputs, mine_grads = barrier((parts_inputs, mine_grads))
    mine, send = call(
        sum_x_kernel,
        "sum_x",
        [((64, units), f32)] * 2,
        [index, own_inputs] + list(parts_inputs),
        moved=2**20,
        scalars=1,
    )
    hidden, slope = call(
        activation_kernel,
        "activation",
        [((64, units), bf16), ((64, units), f32)],
        [mine, other_z(send)],
        moved=2**20,
    )
    (grad_pre,) = call(
        grad_pre_kernel,
        "grad_pre",
        [((64, units), bf16)],
        [mine_grads] + parts_grads + [slope],
        moved=2**20,
    )
    grad_parts = [from_x(grad_pre, step) for step in steps]
    part_hidden, grad_pre = barrier((other_z(hidden), grad_pre))
    (pair,) = call(
        pair_z_kernel,
        "pair_z",
        [((128, units), bf16)],
        [index, hidden, part_hidden],
        moved=2**19,
        scalars=1,
    )
    hidden_pieces = [pair] + [from_x(pair, step) for step in steps]
    grad_parts, pair = barrier((grad_parts, pair))
    stacks = call(
        stack_two_kernel,
        "grad_stack",
        [((128, units), bf16)] * 2,
        [grad_pre] + list(grad_parts),
        moved=2**20,
    )
    hidden_all, far_hidden = units_far(
        far_hidden_kernel, "far_hidden", index, hidden_pieces, w_out, False
    )
    grad_pre_all, far_grad = units_far(
        far_grad_kernel,
        "far_grad",
        index,
        list(stacks) + [other_z(half) for half in stacks],
        w_in,
        True,
    )
    mine_hidden, parts_hidden = units_near(0, hidden_all, w_out, far_hidden)
    mine_grad, parts_grad = units_near(1, grad_pre_all, w_in, far_grad)
    mine, *sends = call(
        column_kernel,
        "column_sums",
        [((32, width), f32)] + [((32, width), bf16)] * 3,
        [mine_hidden] + parts_hidden + [mine_grad] + parts_grad,
        moved=2 * 2**20,
    )
    output, grad_inputs = call(
        last_kernel,
        "last_sums",
        [((16, width), bf16)] * 2,
        [mine] + [to_gx(send, step) for step, send in zip(steps, sends)],
        moved=2**19,
    )
    grad_w_out = lax.dot_general(
        hidden_all, all_grads, (((0,), (0,)), ((), ())), preferred_element_type=f32
    ).astype(bf16)
    grad_w_in = lax.dot_general(
        all_inputs, grad_pre_all, (((0,), (0,)), ((), ())), preferred_element_type=f32
    ).astype(bf16)
    return (output, grad_inputs, grad_w_in, grad_w_out)


def solution(mesh):
    in_specs = (
        P(("gx", "gy"), "gz"),
        P("gz", ("gx", "gy")),
        P(("gx", "gy"), "gz"),
        P(("gx", "gy"), "gz"),
    )
    out_specs = (
        P(("gx", "gy"), "gz"),
        P(("gx", "gy"), "gz"),
        P("gz", ("gx", "gy")),
        P(("gx", "gy"), "gz"),
    )
    return jax.shard_map(
        on_device, mesh=mesh, in_specs=in_specs, out_specs=out_specs, check_vma=False
    )
```

```python
import functools

import jax
import jax.numpy as jnp
from jax import lax
from jax.experimental import pallas as pl
from jax.experimental.pallas import tpu as pltpu
from jax.sharding import PartitionSpec as P

gelu_scale = 0.7978845608028654
cubic_term = 0.044715
tile = 256
bf16 = jnp.bfloat16
f32 = jnp.float32


def gelu_parts(value):
    inner = gelu_scale * (value + cubic_term * value * value * value)
    tanh_part = jnp.tanh(inner)
    result = 0.5 * value * (1.0 + tanh_part)
    slope = 0.5 * (1.0 + tanh_part) + 0.5 * value * (1.0 - tanh_part * tanh_part) * gelu_scale * (
        1.0 + 3.0 * cubic_term * value * value
    )
    return (result, slope)


barrier = lax.optimization_barrier


def from_gx(value, step):
    return lax.ppermute(value, "gx", [((i + step) % 4, i) for i in range(4)])


def to_gx(value, step):
    return lax.ppermute(value, "gx", [(i, (i + step) % 4) for i in range(4)])


def other_core(value):
    return lax.ppermute(value, "gy", [(i, i ^ 1) for i in range(8)])


def from_y(value, step):
    return lax.ppermute(value, "gy", [((i + 2 * step) % 8, i) for i in range(8)])


def to_y(value, step):
    return lax.ppermute(value, "gy", [(i, (i + 2 * step) % 8) for i in range(8)])


def from_x(value, step):
    return lax.ppermute(value, "gz", [((i + 2 * step) % 8, i) for i in range(8)])


def to_x(value, step):
    return lax.ppermute(value, "gz", [(i, (i + 2 * step) % 8) for i in range(8)])


def other_z(value):
    return lax.ppermute(value, "gz", [(i, i ^ 1) for i in range(8)])


def product(left, right, transposed):
    dims = (((1,), (1,)), ((), ())) if transposed else (((1,), (0,)), ((), ()))
    return lax.dot_general(left, right, dims, preferred_element_type=f32)


def columns_of(weight_ref, start, transposed):
    if transposed:
        return weight_ref[pl.ds(start, tile), :]
    return weight_ref[:, pl.ds(start, tile)]


def call(kernel, name, outs, args, scratch=(), moved=0, scalars=0, aliases=None):
    vmem = pl.BlockSpec(memory_space=pltpu.VMEM)
    return pl.pallas_call(
        kernel,
        out_shape=[jax.ShapeDtypeStruct(*out) for out in outs],
        in_specs=[pl.BlockSpec(memory_space=pltpu.SMEM)] * scalars + [vmem] * (len(args) - scalars),
        out_specs=[vmem] * len(outs),
        scratch_shapes=[pltpu.VMEM(*shape) for shape in scratch],
        input_output_aliases=aliases or {},
        compiler_params=pltpu.CompilerParams(vmem_limit_bytes=8 * 2**20),
        cost_estimate=pl.CostEstimate(flops=0, bytes_accessed=moved, transcendentals=0),
        name=name,
    )(*args)


def pair_kernel(inputs_ref, grads_ref, both_ref):
    both_ref[:16, :] = inputs_ref[...]
    both_ref[16:, :] = grads_ref[...]


def columns_kernel(both_ref, first_ref, second_ref, third_ref, inputs_ref, grads_ref):
    for i, source in enumerate((both_ref, first_ref, second_ref, third_ref)):
        inputs_ref[16 * i : 16 * i + 16, :] = source[:16, :]
        grads_ref[16 * i : 16 * i + 16, :] = source[16:, :]


def stack_kernel(*refs):
    rows = refs[0].shape[0]
    for i, piece in enumerate(refs[:4]):
        refs[4][rows * i : rows * (i + 1), :] = piece[...]


def stack(pieces, name):
    rows, width = pieces[0].shape
    return call(stack_kernel, name, [((4 * rows, width), bf16)], pieces, moved=2**20)[0]


def place(index_ref):
    me = index_ref[0]
    return lax.shift_right_logical(me, 1), lax.bitwise_and(me, 1)


def block(x, step, size, offset=0):
    return pl.ds(pl.multiple_of(lax.bitwise_and(x + step, 3) * 128 + offset, 64), size)


def width_inputs_kernel(index_ref, near_ref, far_ref, weight_ref, *refs):
    whole_ref, own_ref, sends, acc = refs[0], refs[1], refs[2:5], refs[5]
    x, z = place(index_ref)
    whole_ref[:256, :] = near_ref[...]
    whole_ref[256:, :] = far_ref[...]

    @pl.loop(0, own_ref.shape[1] // tile)
    def _(j):
        start = pl.multiple_of(j * tile, tile)
        cols = pl.ds(start, tile)
        acc[...] = product(whole_ref[...], columns_of(weight_ref, start, False), False)
        own_ref[:, cols] = acc[block(x, 0, 128), :]
        for step in (1, 2, 3):
            sends[step - 1][:, cols] = acc[block(x, step, 128), :].astype(bf16)


def width_grad_kernel(index_ref, near_ref, far_ref, weight_ref, *refs):
    whole_ref, own_ref, acc = refs[0], refs[1], refs[4]
    x, z = place(index_ref)
    whole_ref[:256, :] = near_ref[...]
    whole_ref[256:, :] = far_ref[...]

    @pl.loop(0, own_ref.shape[1] // tile)
    def _(j):
        start = pl.multiple_of(j * tile, tile)
        cols = pl.ds(start, tile)
        acc[...] = product(whole_ref[...], columns_of(weight_ref, start, True), True)
        for step in range(4):
            rows = slice(64 * step, 64 * step + 64)
            half = slice(64 * (step % 2), 64 * (step % 2) + 64)
            own_ref[rows, cols] = acc[block(x, step, 64, 64 * z), :]
            refs[2 + step // 2][half, cols] = acc[block(x, step, 64, 64 * (1 - z)), :].astype(bf16)


def sum_x_kernel(index_ref, own_ref, first_ref, second_ref, third_ref, mine_ref, send_ref):
    x, z = place(index_ref)
    for target, half in ((mine_ref, z), (send_ref, 1 - z)):

        @pl.loop(0, 4)
        def _(j):
            rows = pl.ds(pl.multiple_of(64 * half + 16 * j, 16), 16)
            total = own_ref[rows, :]
            for piece in (first_ref, second_ref, third_ref):
                total = total + piece[rows, :].astype(f32)
            target[pl.ds(pl.multiple_of(16 * j, 16), 16), :] = total


def activation_kernel(mine_ref, part_ref, hidden_ref, slope_ref):
    @pl.loop(0, 4)
    def _(j):
        rows = pl.ds(pl.multiple_of(16 * j, 16), 16)
        result, slope = gelu_parts(mine_ref[rows, :] + part_ref[rows, :])
        hidden_ref[rows, :] = result.astype(bf16)
        slope_ref[rows, :] = slope


def sum_z_kernel(own_ref, first_ref, second_ref, mine_ref, *sends):
    for step in range(4):

        @pl.loop(0, 4)
        def _(j):
            rows = pl.ds(pl.multiple_of(64 * step + 16 * j, 16), 16)
            local = pl.ds(pl.multiple_of(16 * j, 16), 16)
            part = (first_ref, second_ref)[step // 2]
            half = pl.ds(pl.multiple_of(64 * (step % 2) + 16 * j, 16), 16)
            total = own_ref[rows, :] + part[half, :].astype(f32)
            if step == 0:
                mine_ref[local, :] = total
            else:
                sends[step - 1][local, :] = total.astype(bf16)


def grad_pre_kernel(mine_ref, first_ref, second_ref, third_ref, slope_ref, out_ref):
    @pl.loop(0, 4)
    def _(j):
        rows = pl.ds(pl.multiple_of(16 * j, 16), 16)
        total = mine_ref[rows, :]
        for piece in (first_ref, second_ref, third_ref):
            total = total + piece[rows, :].astype(f32)
        out_ref[rows, :] = (total * slope_ref[rows, :]).astype(bf16)


def pair_z_kernel(index_ref, own_ref, part_ref, out_ref):
    x, z = place(index_ref)
    out_ref[pl.ds(pl.multiple_of(64 * z, 64), 64), :] = own_ref[...]
    out_ref[pl.ds(pl.multiple_of(64 * (1 - z), 64), 64), :] = part_ref[...]


def far_columns(whole_ref, weight_ref, far_ref, transposed):
    @pl.loop(0, far_ref.shape[1] // tile)
    def _(j):
        start = pl.multiple_of(j * tile, tile)
        far_ref[:, pl.ds(start, tile)] = product(
            whole_ref[256:, :], columns_of(weight_ref, start, transposed), transposed
        )


def far_hidden_kernel(index_ref, *refs):
    pieces, weight_ref, whole_ref, far_ref = refs[:4], refs[4], refs[5], refs[6]
    x, z = place(index_ref)
    for step in range(4):
        whole_ref[block(x, step, 128), :] = pieces[step][...]
    far_columns(whole_ref, weight_ref, far_ref, False)


def far_grad_kernel(index_ref, own_ref, part_ref, weight_ref, whole_ref, far_ref):
    x, z = place(index_ref)
    for step in range(4):
        rows = slice(64 * step, 64 * step + 64)
        whole_ref[block(x, step, 64, 64 * z), :] = own_ref[rows, :]
        whole_ref[block(x, step, 64, 64 * (1 - z)), :] = part_ref[rows, :]
    far_columns(whole_ref, weight_ref, far_ref, True)


def near_kernel(transposed, whole_ref, weight_ref, far_ref, mine_ref, *refs):
    sends, acc = refs[:3], refs[3]

    @pl.loop(0, mine_ref.shape[1] // tile)
    def _(j):
        start = pl.multiple_of(j * tile, tile)
        cols = pl.ds(start, tile)
        acc[...] = far_ref[:, cols] + product(
            whole_ref[:256, :], columns_of(weight_ref, start, transposed), transposed
        )
        mine_ref[:, cols] = acc[:64, :]
        for step in (1, 2, 3):
            sends[step - 1][:, cols] = acc[64 * step : 64 * step + 64, :].astype(bf16)


def column_kernel(*refs):
    mine_ref, sends = refs[8], refs[9:12]
    for step in range(4):
        rows = slice(16 * step, 16 * step + 16)
        for part in range(2):
            total = refs[4 * part][rows, :]
            for piece in refs[4 * part + 1 : 4 * part + 4]:
                total = total + piece[rows, :].astype(f32)
            if step == 0:
                mine_ref[16 * part : 16 * part + 16, :] = total
            else:
                sends[step - 1][16 * part : 16 * part + 16, :] = total.astype(bf16)


def last_kernel(mine_ref, first_ref, second_ref, third_ref, *outs):
    for part, out in enumerate(outs):
        rows = slice(16 * part, 16 * part + 16)
        total = mine_ref[rows, :]
        for piece in (first_ref, second_ref, third_ref):
            total = total + piece[rows, :].astype(f32)
        out[...] = total.astype(bf16)


def units_far(kernel, name, index, pieces, weight, transposed):
    units = pieces[0].shape[1]
    width = weight.shape[0] if transposed else weight.shape[1]
    whole, far = call(
        kernel,
        name,
        [((512, units), bf16), ((256, width), f32)],
        [index] + pieces + [weight],
        moved=6 * 2**20,
        scalars=1,
    )
    return whole, other_core(far)


def units_near(part, whole, weight, far):
    units, width = whole.shape[1], far.shape[1]
    mine, *sends = call(
        functools.partial(near_kernel, bool(part)),
        "near_grad" if part else "near_hidden",
        [((64, width), f32)] + [((64, width), bf16)] * 3,
        [whole, weight, far],
        scratch=[((256, tile), f32)],
        moved=6 * 2**20,
    )
    return mine, [to_y(send, step) for step, send in zip((1, 2, 3), sends)]


def on_device(inputs, w_in, w_out, grad_out):
    width, units = w_in.shape
    index = jnp.reshape(lax.axis_index("gz"), (1,)).astype(jnp.int32)
    steps = (1, 2, 3)
    (both,) = call(pair_kernel, "pair", [((32, width), bf16)], [inputs, grad_out], moved=2**18)
    columns = call(
        columns_kernel,
        "columns",
        [((64, width), bf16)] * 2,
        [both] + [from_gx(both, step) for step in steps],
        moved=2**20,
    )
    planes = [[column] + [from_y(column, step) for step in steps] for column in columns]
    near = stack(planes[0], "plane")
    all_inputs, own, *sends = call(
        width_inputs_kernel,
        "width_inputs",
        [((512, width), bf16), ((128, units), f32)] + [((128, units), bf16)] * 3,
        [index, near, other_core(near), w_in],
        scratch=[((512, tile), f32)],
        moved=6 * 2**20,
        scalars=1,
    )
    own_inputs, parts_inputs = own, [to_x(send, step) for step, send in zip(steps, sends)]
    plane, own_inputs = barrier((planes[1], own_inputs))
    near = stack(plane, "plane")
    all_grads, own, *halves = call(
        width_grad_kernel,
        "width_grad",
        [((512, width), bf16), ((256, units), f32)] + [((128, units), bf16)] * 2,
        [index, near, other_core(near), w_out],
        scratch=[((512, tile), f32)],
        moved=6 * 2**20,
        scalars=1,
    )
    mine_inputs, send_inputs = call(
        sum_x_kernel,
        "sum_x",
        [((64, units), f32)] * 2,
        [index, own_inputs] + parts_inputs,
        moved=2**20,
        scalars=1,
    )
    hidden, slope = call(
        activation_kernel,
        "activation",
        [((64, units), bf16), ((64, units), f32)],
        [mine_inputs, other_z(send_inputs)],
        moved=2**20,
    )
    mine, *sends = call(
        sum_z_kernel,
        "sum_z",
        [((64, units), f32)] + [((64, units), bf16)] * 3,
        [own] + [other_z(half) for half in halves],
        moved=2**20,
    )
    (pair,) = call(
        pair_z_kernel,
        "pair_z",
        [((128, units), bf16)],
        [index, hidden, other_z(hidden)],
        moved=2**19,
        scalars=1,
    )
    (grad_pre,) = call(
        grad_pre_kernel,
        "grad_pre",
        [((64, units), bf16)],
        [mine] + [to_x(send, step) for step, send in zip(steps, sends)] + [slope],
        moved=2**20,
    )
    hidden_pieces = [pair] + [from_x(pair, step) for step in steps]
    grad_stack = stack([grad_pre] + [from_x(grad_pre, step) for step in steps], "grad_stack")
    hidden_all, far_hidden = units_far(
        far_hidden_kernel, "far_hidden", index, hidden_pieces, w_out, False
    )
    grad_pre_all, far_grad = units_far(
        far_grad_kernel, "far_grad", index, [grad_stack, other_z(grad_stack)], w_in, True
    )
    mine_hidden, parts_hidden = units_near(0, hidden_all, w_out, far_hidden)
    mine_grad, parts_grad = units_near(1, grad_pre_all, w_in, far_grad)
    mine, *sends = call(
        column_kernel,
        "column_sums",
        [((32, width), f32)] + [((32, width), bf16)] * 3,
        [mine_hidden] + parts_hidden + [mine_grad] + parts_grad,
        moved=2 * 2**20,
    )
    output, grad_inputs = call(
        last_kernel,
        "last_sums",
        [((16, width), bf16)] * 2,
        [mine] + [to_gx(send, step) for step, send in zip(steps, sends)],
        moved=2**19,
    )
    grad_w_out = lax.dot_general(
        hidden_all, all_grads, (((0,), (0,)), ((), ())), preferred_element_type=f32
    ).astype(bf16)
    grad_w_in = lax.dot_general(
        all_inputs, grad_pre_all, (((0,), (0,)), ((), ())), preferred_element_type=f32
    ).astype(bf16)
    return (output, grad_inputs, grad_w_in, grad_w_out)


def solution(mesh):
    in_specs = (
        P(("gx", "gy"), "gz"),
        P("gz", ("gx", "gy")),
        P(("gx", "gy"), "gz"),
        P(("gx", "gy"), "gz"),
    )
    out_specs = (
        P(("gx", "gy"), "gz"),
        P(("gx", "gy"), "gz"),
        P("gz", ("gx", "gy")),
        P(("gx", "gy"), "gz"),
    )
    return jax.shard_map(
        on_device, mesh=mesh, in_specs=in_specs, out_specs=out_specs, check_vma=False
    )
```

```python
import functools

import jax
import jax.numpy as jnp
from jax import lax
from jax.experimental import pallas as pl
from jax.experimental.pallas import tpu as pltpu
from jax.sharding import PartitionSpec as P

gelu_scale = 0.7978845608028654
cubic_term = 0.044715
tile = 256
bf16 = jnp.bfloat16
f32 = jnp.float32


def gelu_parts(value):
    inner = gelu_scale * (value + cubic_term * value * value * value)
    tanh_part = jnp.tanh(inner)
    result = 0.5 * value * (1.0 + tanh_part)
    slope = 0.5 * (1.0 + tanh_part) + 0.5 * value * (1.0 - tanh_part * tanh_part) * gelu_scale * (
        1.0 + 3.0 * cubic_term * value * value
    )
    return (result, slope)


barrier = lax.optimization_barrier


def from_gx(value, step):
    return lax.ppermute(value, "gx", [((i + step) % 4, i) for i in range(4)])


def to_gx(value, step):
    return lax.ppermute(value, "gx", [(i, (i + step) % 4) for i in range(4)])


def other_core(value):
    return lax.ppermute(value, "gy", [(i, i ^ 1) for i in range(8)])


def from_y(value, step):
    return lax.ppermute(value, "gy", [((i + 2 * step) % 8, i) for i in range(8)])


def to_y(value, step):
    return lax.ppermute(value, "gy", [(i, (i + 2 * step) % 8) for i in range(8)])


def from_x(value, step):
    return lax.ppermute(value, "gz", [((i + 2 * step) % 8, i) for i in range(8)])


def to_x(value, step):
    return lax.ppermute(value, "gz", [(i, (i + 2 * step) % 8) for i in range(8)])


def other_z(value):
    return lax.ppermute(value, "gz", [(i, i ^ 1) for i in range(8)])


def product(left, right, transposed):
    dims = (((1,), (1,)), ((), ())) if transposed else (((1,), (0,)), ((), ()))
    return lax.dot_general(left, right, dims, preferred_element_type=f32)


def columns_of(weight_ref, start, transposed):
    if transposed:
        return weight_ref[pl.ds(start, tile), :]
    return weight_ref[:, pl.ds(start, tile)]


def call(kernel, name, outs, args, scratch=(), flops=0, moved=0, scalars=0, aliases=None):
    vmem = pl.BlockSpec(memory_space=pltpu.VMEM)
    return pl.pallas_call(
        kernel,
        out_shape=[jax.ShapeDtypeStruct(*out) for out in outs],
        in_specs=[pl.BlockSpec(memory_space=pltpu.SMEM)] * scalars + [vmem] * (len(args) - scalars),
        out_specs=[vmem] * len(outs),
        scratch_shapes=[pltpu.VMEM(*shape) for shape in scratch],
        input_output_aliases=aliases or {},
        compiler_params=pltpu.CompilerParams(vmem_limit_bytes=8 * 2**20),
        cost_estimate=pl.CostEstimate(flops=flops, bytes_accessed=moved, transcendentals=0),
        name=name,
    )(*args)


def pair_kernel(inputs_ref, grads_ref, both_ref, sems):
    copies = [
        pltpu.make_async_copy(source, both_ref.at[pl.ds(16 * i, 16), :], sems.at[i])
        for i, source in enumerate((inputs_ref, grads_ref))
    ]
    for copy in copies:
        copy.start()
    for copy in copies:
        copy.wait()


def pair(inputs, grads):
    return pl.pallas_call(
        pair_kernel,
        out_shape=jax.ShapeDtypeStruct((32, inputs.shape[1]), bf16),
        in_specs=[pl.BlockSpec(memory_space=pl.ANY)] * 2,
        out_specs=pl.BlockSpec(memory_space=pltpu.VMEM),
        scratch_shapes=[pltpu.SemaphoreType.DMA((2,))],
        name="pair",
    )(inputs, grads)


def columns_kernel(both_ref, first_ref, second_ref, third_ref, inputs_ref, grads_ref):
    for i, source in enumerate((both_ref, first_ref, second_ref, third_ref)):
        inputs_ref[16 * i : 16 * i + 16, :] = source[:16, :]
        grads_ref[16 * i : 16 * i + 16, :] = source[16:, :]


def stack_kernel(*refs):
    rows = refs[0].shape[0]
    for i, piece in enumerate(refs[:4]):
        refs[4][rows * i : rows * (i + 1), :] = piece[...]


def stack(pieces, name):
    rows, width = pieces[0].shape
    return call(stack_kernel, name, [((4 * rows, width), bf16)], pieces, moved=2**20)[0]


def place(index_ref):
    me = index_ref[0]
    return lax.shift_right_logical(me, 1), lax.bitwise_and(me, 1)


def block(x, step, size, offset=0):
    return pl.ds(pl.multiple_of(lax.bitwise_and(x + step, 3) * 128 + offset, 64), size)


def width_inputs_kernel(index_ref, near_ref, far_ref, weight_ref, *refs):
    whole_ref, own_ref, sends, acc = refs[0], refs[1], refs[2:5], refs[5]
    x, z = place(index_ref)
    whole_ref[:256, :] = near_ref[...]
    whole_ref[256:, :] = far_ref[...]

    @pl.loop(0, own_ref.shape[1] // tile)
    def _(j):
        start = pl.multiple_of(j * tile, tile)
        cols = pl.ds(start, tile)
        acc[...] = product(whole_ref[...], columns_of(weight_ref, start, False), False)
        own_ref[:, cols] = acc[block(x, 0, 128), :]
        for step in (1, 2, 3):
            sends[step - 1][:, cols] = acc[block(x, step, 128), :].astype(bf16)


def width_grad_kernel(index_ref, near_ref, far_ref, weight_ref, *refs):
    whole_ref, own_ref, send_ref, acc = refs
    x, z = place(index_ref)
    whole_ref[:256, :] = near_ref[...]
    whole_ref[256:, :] = far_ref[...]

    @pl.loop(0, own_ref.shape[1] // tile)
    def _(j):
        start = pl.multiple_of(j * tile, tile)
        cols = pl.ds(start, tile)
        acc[...] = product(whole_ref[...], columns_of(weight_ref, start, True), True)
        for step in range(4):
            rows = slice(64 * step, 64 * step + 64)
            own_ref[rows, cols] = acc[block(x, step, 64, 64 * z), :]
            send_ref[rows, cols] = acc[block(x, step, 64, 64 * (1 - z)), :].astype(bf16)


def sum_x_kernel(index_ref, own_ref, first_ref, second_ref, third_ref, mine_ref, send_ref):
    x, z = place(index_ref)
    for target, half in ((mine_ref, z), (send_ref, 1 - z)):

        @pl.loop(0, 4)
        def _(j):
            rows = pl.ds(pl.multiple_of(64 * half + 16 * j, 16), 16)
            total = own_ref[rows, :]
            for piece in (first_ref, second_ref, third_ref):
                total = total + piece[rows, :].astype(f32)
            target[pl.ds(pl.multiple_of(16 * j, 16), 16), :] = total


def activation_kernel(mine_ref, part_ref, hidden_ref, slope_ref):
    @pl.loop(0, 4)
    def _(j):
        rows = pl.ds(pl.multiple_of(16 * j, 16), 16)
        result, slope = gelu_parts(mine_ref[rows, :] + part_ref[rows, :])
        hidden_ref[rows, :] = result.astype(bf16)
        slope_ref[rows, :] = slope


def sum_z_kernel(own_ref, part_ref, mine_ref, *sends):
    for step in range(4):

        @pl.loop(0, 4)
        def _(j):
            rows = pl.ds(pl.multiple_of(64 * step + 16 * j, 16), 16)
            local = pl.ds(pl.multiple_of(16 * j, 16), 16)
            total = own_ref[rows, :] + part_ref[rows, :].astype(f32)
            if step == 0:
                mine_ref[local, :] = total
            else:
                sends[step - 1][local, :] = total.astype(bf16)


def grad_pre_kernel(mine_ref, first_ref, second_ref, third_ref, slope_ref, out_ref):
    @pl.loop(0, 4)
    def _(j):
        rows = pl.ds(pl.multiple_of(16 * j, 16), 16)
        total = mine_ref[rows, :]
        for piece in (first_ref, second_ref, third_ref):
            total = total + piece[rows, :].astype(f32)
        out_ref[rows, :] = (total * slope_ref[rows, :]).astype(bf16)


def pair_z_kernel(index_ref, own_ref, part_ref, out_ref):
    x, z = place(index_ref)
    out_ref[pl.ds(pl.multiple_of(64 * z, 64), 64), :] = own_ref[...]
    out_ref[pl.ds(pl.multiple_of(64 * (1 - z), 64), 64), :] = part_ref[...]


def far_columns(whole_ref, weight_ref, far_ref, transposed):
    @pl.loop(0, far_ref.shape[1] // tile)
    def _(j):
        start = pl.multiple_of(j * tile, tile)
        far_ref[:, pl.ds(start, tile)] = product(
            whole_ref[256:, :], columns_of(weight_ref, start, transposed), transposed
        )


def far_hidden_kernel(index_ref, *refs):
    pieces, weight_ref, whole_ref, far_ref = refs[:4], refs[4], refs[5], refs[6]
    x, z = place(index_ref)
    for step in range(4):
        whole_ref[block(x, step, 128), :] = pieces[step][...]
    far_columns(whole_ref, weight_ref, far_ref, False)


def far_grad_kernel(index_ref, own_ref, part_ref, weight_ref, whole_ref, far_ref):
    x, z = place(index_ref)
    for step in range(4):
        rows = slice(64 * step, 64 * step + 64)
        whole_ref[block(x, step, 64, 64 * z), :] = own_ref[rows, :]
        whole_ref[block(x, step, 64, 64 * (1 - z)), :] = part_ref[rows, :]
    far_columns(whole_ref, weight_ref, far_ref, True)


def near_kernel(transposed, whole_ref, weight_ref, far_ref, mine_ref, *refs):
    sends, acc = refs[:3], refs[3]

    @pl.loop(0, mine_ref.shape[1] // tile)
    def _(j):
        start = pl.multiple_of(j * tile, tile)
        cols = pl.ds(start, tile)
        acc[...] = far_ref[:, cols] + product(
            whole_ref[:256, :], columns_of(weight_ref, start, transposed), transposed
        )
        mine_ref[:, cols] = acc[:64, :]
        for step in (1, 2, 3):
            sends[step - 1][:, cols] = acc[64 * step : 64 * step + 64, :].astype(bf16)


def column_kernel(*refs):
    mine_ref, sends = refs[4], refs[5:8]
    for step in range(4):
        rows = slice(16 * step, 16 * step + 16)
        total = refs[0][rows, :]
        for piece in refs[1:4]:
            total = total + piece[rows, :].astype(f32)
        if step == 0:
            mine_ref[...] = total
        else:
            sends[step - 1][...] = total.astype(bf16)


def last_kernel(mine_ref, first_ref, second_ref, third_ref, out_ref):
    total = mine_ref[...]
    for piece in (first_ref, second_ref, third_ref):
        total = total + piece[...].astype(f32)
    out_ref[...] = total.astype(bf16)


def column_sum(mine, parts):
    width = mine.shape[1]
    mine, *sends = call(
        column_kernel,
        "column_sum",
        [((16, width), f32)] + [((16, width), bf16)] * 3,
        [mine] + list(parts),
        moved=2**20,
    )
    return mine, [to_gx(send, step) for step, send in zip((1, 2, 3), sends)]


def last_sum(mine, parts):
    return call(last_kernel, "last_sum", [(mine.shape, bf16)], [mine] + list(parts), moved=2**18)[0]


def units_far(kernel, name, index, pieces, weight, transposed):
    units = pieces[0].shape[1]
    width = weight.shape[0] if transposed else weight.shape[1]
    whole, far = call(
        kernel,
        name,
        [((512, units), bf16), ((256, width), f32)],
        [index] + pieces + [weight],
        flops=2 * 256 * width * units,
        moved=6 * 2**20,
        scalars=1,
    )
    return whole, other_core(far)


def units_near(part, whole, weight, far):
    units, width = whole.shape[1], far.shape[1]
    mine, *sends = call(
        functools.partial(near_kernel, bool(part)),
        "near_grad" if part else "near_hidden",
        [((64, width), f32)] + [((64, width), bf16)] * 3,
        [whole, weight, far],
        scratch=[((256, tile), f32)],
        flops=2 * 256 * width * units,
        moved=6 * 2**20,
    )
    return mine, [to_y(send, step) for step, send in zip((1, 2, 3), sends)]


def on_device(inputs, w_in, w_out, grad_out):
    width, units = w_in.shape
    index = jnp.reshape(lax.axis_index("gz"), (1,)).astype(jnp.int32)
    steps = (1, 2, 3)
    both = pair(inputs, grad_out)
    columns = call(
        columns_kernel,
        "columns",
        [((64, width), bf16)] * 2,
        [both] + [from_gx(both, step) for step in steps],
        moved=2**20,
    )
    planes = [[column] + [from_y(column, step) for step in steps] for column in columns]
    near = stack(planes[0], "plane")
    width_flops = 2 * 512 * width * units
    all_inputs, own, *sends = call(
        width_inputs_kernel,
        "width_inputs",
        [((512, width), bf16), ((128, units), f32)] + [((128, units), bf16)] * 3,
        [index, near, other_core(near), w_in],
        scratch=[((512, tile), f32)],
        flops=width_flops,
        moved=6 * 2**20,
        scalars=1,
    )
    mine, send = call(
        sum_x_kernel,
        "sum_x",
        [((64, units), f32)] * 2,
        [index, own] + [to_x(send, step) for step, send in zip(steps, sends)],
        moved=2**20,
        scalars=1,
    )
    hidden, slope = call(
        activation_kernel,
        "activation",
        [((64, units), bf16), ((64, units), f32)],
        [mine, other_z(send)],
        moved=2**20,
    )
    near = stack(planes[1], "plane")
    all_grads, own, send = call(
        width_grad_kernel,
        "width_grad",
        [((512, width), bf16), ((256, units), f32), ((256, units), bf16)],
        [index, near, other_core(near), w_out],
        scratch=[((512, tile), f32)],
        flops=width_flops,
        moved=6 * 2**20,
        scalars=1,
    )
    mine, *sends = call(
        sum_z_kernel,
        "sum_z",
        [((64, units), f32)] + [((64, units), bf16)] * 3,
        [own, other_z(send)],
        moved=2**20,
    )
    (both_z,) = call(
        pair_z_kernel,
        "pair_z",
        [((128, units), bf16)],
        [index, hidden, other_z(hidden)],
        moved=2**19,
        scalars=1,
    )
    (grad_pre,) = call(
        grad_pre_kernel,
        "grad_pre",
        [((64, units), bf16)],
        [mine] + [to_x(send, step) for step, send in zip(steps, sends)] + [slope],
        moved=2**20,
    )
    hidden_pieces = [both_z] + [from_x(both_z, step) for step in steps]
    grad_stack = stack([grad_pre] + [from_x(grad_pre, step) for step in steps], "grad_stack")
    hidden_all, far_hidden = units_far(
        far_hidden_kernel, "far_hidden", index, hidden_pieces, w_out, False
    )
    grad_pre_all, far_grad = units_far(
        far_grad_kernel, "far_grad", index, [grad_stack, other_z(grad_stack)], w_in, True
    )
    mine_hidden, parts_hidden = units_near(0, hidden_all, w_out, far_hidden)
    mine_grad, parts_grad = units_near(1, grad_pre_all, w_in, far_grad)
    grad_w_out = lax.dot_general(
        hidden_all, all_grads, (((0,), (0,)), ((), ())), preferred_element_type=f32
    ).astype(bf16)
    grad_w_in = lax.dot_general(
        all_inputs, grad_pre_all, (((0,), (0,)), ((), ())), preferred_element_type=f32
    ).astype(bf16)
    parts_hidden, grad_w_out = barrier((parts_hidden, grad_w_out))
    mine_hidden, ends_hidden = column_sum(mine_hidden, parts_hidden)
    mine_grad, ends_grad = column_sum(mine_grad, parts_grad)
    ends_hidden, mine_grad = barrier((ends_hidden, mine_grad))
    output = last_sum(mine_hidden, ends_hidden)
    grad_inputs = last_sum(mine_grad, ends_grad)
    return (output, grad_inputs, grad_w_in, grad_w_out)


def solution(mesh):
    in_specs = (
        P(("gx", "gy"), "gz"),
        P("gz", ("gx", "gy")),
        P(("gx", "gy"), "gz"),
        P(("gx", "gy"), "gz"),
    )
    out_specs = (
        P(("gx", "gy"), "gz"),
        P(("gx", "gy"), "gz"),
        P("gz", ("gx", "gy")),
        P(("gx", "gy"), "gz"),
    )
    return jax.shard_map(
        on_device, mesh=mesh, in_specs=in_specs, out_specs=out_specs, check_vma=False
    )
```

```python
import functools

import jax
import jax.numpy as jnp
from jax import lax
from jax.experimental import pallas as pl
from jax.experimental.pallas import tpu as pltpu
from jax.sharding import PartitionSpec as P

gelu_scale = 0.7978845608028654
cubic_term = 0.044715
tile = 256
bf16 = jnp.bfloat16
f32 = jnp.float32


def gelu_parts(value):
    inner = gelu_scale * (value + cubic_term * value * value * value)
    tanh_part = jnp.tanh(inner)
    result = 0.5 * value * (1.0 + tanh_part)
    slope = 0.5 * (1.0 + tanh_part) + 0.5 * value * (1.0 - tanh_part * tanh_part) * gelu_scale * (
        1.0 + 3.0 * cubic_term * value * value
    )
    return (result, slope)


barrier = lax.optimization_barrier


def from_gx(value, step):
    return lax.ppermute(value, "gx", [((i + step) % 4, i) for i in range(4)])


def to_gx(value, step):
    return lax.ppermute(value, "gx", [(i, (i + step) % 4) for i in range(4)])


def other_core(value):
    return lax.ppermute(value, "gy", [(i, i ^ 1) for i in range(8)])


def from_y(value, step):
    return lax.ppermute(value, "gy", [((i + 2 * step) % 8, i) for i in range(8)])


def to_y(value, step):
    return lax.ppermute(value, "gy", [(i, (i + 2 * step) % 8) for i in range(8)])


def from_x(value, step):
    return lax.ppermute(value, "gz", [((i + 2 * step) % 8, i) for i in range(8)])


def to_x(value, step):
    return lax.ppermute(value, "gz", [(i, (i + 2 * step) % 8) for i in range(8)])


def other_z(value):
    return lax.ppermute(value, "gz", [(i, i ^ 1) for i in range(8)])


def product(left, right, transposed):
    dims = (((1,), (1,)), ((), ())) if transposed else (((1,), (0,)), ((), ()))
    return lax.dot_general(left, right, dims, preferred_element_type=f32)


def columns_of(weight_ref, start, transposed):
    if transposed:
        return weight_ref[pl.ds(start, tile), :]
    return weight_ref[:, pl.ds(start, tile)]


def call(kernel, name, outs, args, scratch=(), flops=0, moved=0, scalars=0, aliases=None):
    vmem = pl.BlockSpec(memory_space=pltpu.VMEM)
    return pl.pallas_call(
        kernel,
        out_shape=[jax.ShapeDtypeStruct(*out) for out in outs],
        in_specs=[pl.BlockSpec(memory_space=pltpu.SMEM)] * scalars + [vmem] * (len(args) - scalars),
        out_specs=[vmem] * len(outs),
        scratch_shapes=[pltpu.VMEM(*shape) for shape in scratch],
        input_output_aliases=aliases or {},
        compiler_params=pltpu.CompilerParams(vmem_limit_bytes=8 * 2**20),
        cost_estimate=pl.CostEstimate(flops=flops, bytes_accessed=moved, transcendentals=0),
        name=name,
    )(*args)


def pair_kernel(inputs_ref, grads_ref, both_ref):
    both_ref[:16, :] = inputs_ref[...]
    both_ref[16:, :] = grads_ref[...]


def columns_kernel(both_ref, first_ref, second_ref, third_ref, inputs_ref, grads_ref):
    for i, source in enumerate((both_ref, first_ref, second_ref, third_ref)):
        inputs_ref[16 * i : 16 * i + 16, :] = source[:16, :]
        grads_ref[16 * i : 16 * i + 16, :] = source[16:, :]


def stack_kernel(*refs):
    rows = refs[0].shape[0]
    for i, piece in enumerate(refs[:4]):
        refs[4][rows * i : rows * (i + 1), :] = piece[...]


def stack(pieces, name):
    rows, width = pieces[0].shape
    return call(stack_kernel, name, [((4 * rows, width), bf16)], pieces, moved=2**20)[0]


def halves_kernel(*refs):
    for i, piece in enumerate(refs[:4]):
        refs[4 + i // 2][64 * (i % 2) : 64 * (i % 2) + 64, :] = piece[...]


def halves(pieces):
    width = pieces[0].shape[1]
    return list(call(halves_kernel, "plane", [((128, width), bf16)] * 2, pieces, moved=2**20))


def place(index_ref):
    me = index_ref[0]
    return lax.shift_right_logical(me, 1), lax.bitwise_and(me, 1)


def block(x, step, size, offset=0):
    return pl.ds(pl.multiple_of(lax.bitwise_and(x + step, 3) * 128 + offset, 64), size)


def width_inputs_kernel(index_ref, *refs):
    pieces, weight_ref = refs[:4], refs[4]
    whole_ref, own_ref, sends, acc = refs[5], refs[6], refs[7:10], refs[10]
    x, z = place(index_ref)
    for i, piece in enumerate(pieces):
        whole_ref[128 * i : 128 * i + 128, :] = piece[...]

    @pl.loop(0, own_ref.shape[1] // tile)
    def _(j):
        start = pl.multiple_of(j * tile, tile)
        cols = pl.ds(start, tile)
        acc[...] = product(whole_ref[...], columns_of(weight_ref, start, False), False)
        own_ref[:, cols] = acc[block(x, 0, 128), :]
        for step in (1, 2, 3):
            sends[step - 1][:, cols] = acc[block(x, step, 128), :].astype(bf16)


def width_grad_kernel(index_ref, *refs):
    pieces, weight_ref = refs[:4], refs[4]
    whole_ref, own_ref, send_ref, acc = refs[5:]
    x, z = place(index_ref)
    for i, piece in enumerate(pieces):
        whole_ref[128 * i : 128 * i + 128, :] = piece[...]

    @pl.loop(0, own_ref.shape[1] // tile)
    def _(j):
        start = pl.multiple_of(j * tile, tile)
        cols = pl.ds(start, tile)
        acc[...] = product(whole_ref[...], columns_of(weight_ref, start, True), True)
        for step in range(4):
            rows = slice(64 * step, 64 * step + 64)
            own_ref[rows, cols] = acc[block(x, step, 64, 64 * z), :]
            send_ref[rows, cols] = acc[block(x, step, 64, 64 * (1 - z)), :].astype(bf16)


def sum_x_kernel(index_ref, own_ref, first_ref, second_ref, third_ref, mine_ref, send_ref):
    x, z = place(index_ref)
    for target, half in ((mine_ref, z), (send_ref, 1 - z)):

        @pl.loop(0, 4)
        def _(j):
            rows = pl.ds(pl.multiple_of(64 * half + 16 * j, 16), 16)
            total = own_ref[rows, :]
            for piece in (first_ref, second_ref, third_ref):
                total = total + piece[rows, :].astype(f32)
            target[pl.ds(pl.multiple_of(16 * j, 16), 16), :] = total


def activation_kernel(mine_ref, part_ref, hidden_ref, slope_ref):
    @pl.loop(0, 4)
    def _(j):
        rows = pl.ds(pl.multiple_of(16 * j, 16), 16)
        result, slope = gelu_parts(mine_ref[rows, :] + part_ref[rows, :])
        hidden_ref[rows, :] = result.astype(bf16)
        slope_ref[rows, :] = slope


def sum_z_kernel(own_ref, part_ref, mine_ref, *sends):
    for step in range(4):

        @pl.loop(0, 4)
        def _(j):
            rows = pl.ds(pl.multiple_of(64 * step + 16 * j, 16), 16)
            local = pl.ds(pl.multiple_of(16 * j, 16), 16)
            total = own_ref[rows, :] + part_ref[rows, :].astype(f32)
            if step == 0:
                mine_ref[local, :] = total
            else:
                sends[step - 1][local, :] = total.astype(bf16)


def grad_pre_kernel(mine_ref, first_ref, second_ref, third_ref, slope_ref, out_ref):
    @pl.loop(0, 4)
    def _(j):
        rows = pl.ds(pl.multiple_of(16 * j, 16), 16)
        total = mine_ref[rows, :]
        for piece in (first_ref, second_ref, third_ref):
            total = total + piece[rows, :].astype(f32)
        out_ref[rows, :] = (total * slope_ref[rows, :]).astype(bf16)


def pair_z_kernel(index_ref, own_ref, part_ref, out_ref):
    x, z = place(index_ref)
    out_ref[pl.ds(pl.multiple_of(64 * z, 64), 64), :] = own_ref[...]
    out_ref[pl.ds(pl.multiple_of(64 * (1 - z), 64), 64), :] = part_ref[...]


def far_columns(whole_ref, weight_ref, far_ref, transposed):
    @pl.loop(0, far_ref.shape[1] // tile)
    def _(j):
        start = pl.multiple_of(j * tile, tile)
        far_ref[:, pl.ds(start, tile)] = product(
            whole_ref[256:, :], columns_of(weight_ref, start, transposed), transposed
        )


def far_hidden_kernel(index_ref, *refs):
    pieces, weight_ref, whole_ref, far_ref = refs[:4], refs[4], refs[5], refs[6]
    x, z = place(index_ref)
    for step in range(4):
        whole_ref[block(x, step, 128), :] = pieces[step][...]
    far_columns(whole_ref, weight_ref, far_ref, False)


def far_grad_kernel(index_ref, own_ref, part_ref, weight_ref, whole_ref, far_ref):
    x, z = place(index_ref)
    for step in range(4):
        rows = slice(64 * step, 64 * step + 64)
        whole_ref[block(x, step, 64, 64 * z), :] = own_ref[rows, :]
        whole_ref[block(x, step, 64, 64 * (1 - z)), :] = part_ref[rows, :]
    far_columns(whole_ref, weight_ref, far_ref, True)


def near_kernel(transposed, whole_ref, weight_ref, far_ref, mine_ref, *refs):
    sends, acc = refs[:3], refs[3]

    @pl.loop(0, mine_ref.shape[1] // tile)
    def _(j):
        start = pl.multiple_of(j * tile, tile)
        cols = pl.ds(start, tile)
        acc[...] = far_ref[:, cols] + product(
            whole_ref[:256, :], columns_of(weight_ref, start, transposed), transposed
        )
        mine_ref[:, cols] = acc[:64, :]
        for step in (1, 2, 3):
            sends[step - 1][:, cols] = acc[64 * step : 64 * step + 64, :].astype(bf16)


def column_kernel(*refs):
    mine_ref, sends = refs[4], refs[5:8]
    for step in range(4):
        rows = slice(16 * step, 16 * step + 16)
        total = refs[0][rows, :]
        for piece in refs[1:4]:
            total = total + piece[rows, :].astype(f32)
        if step == 0:
            mine_ref[...] = total
        else:
            sends[step - 1][...] = total.astype(bf16)


def last_kernel(mine_ref, first_ref, second_ref, third_ref, out_ref):
    total = mine_ref[...]
    for piece in (first_ref, second_ref, third_ref):
        total = total + piece[...].astype(f32)
    out_ref[...] = total.astype(bf16)


def column_sum(mine, parts):
    width = mine.shape[1]
    mine, *sends = call(
        column_kernel,
        "column_sum",
        [((16, width), f32)] + [((16, width), bf16)] * 3,
        [mine] + list(parts),
        moved=2**20,
    )
    return mine, [to_gx(send, step) for step, send in zip((1, 2, 3), sends)]


def last_sum(mine, parts):
    return call(last_kernel, "last_sum", [(mine.shape, bf16)], [mine] + list(parts), moved=2**18)[0]


def units_far(kernel, name, index, pieces, weight, transposed):
    units = pieces[0].shape[1]
    width = weight.shape[0] if transposed else weight.shape[1]
    whole, far = call(
        kernel,
        name,
        [((512, units), bf16), ((256, width), f32)],
        [index] + pieces + [weight],
        flops=2 * 256 * width * units,
        moved=6 * 2**20,
        scalars=1,
    )
    return whole, other_core(far)


def units_near(part, whole, weight, far):
    units, width = whole.shape[1], far.shape[1]
    mine, *sends = call(
        functools.partial(near_kernel, bool(part)),
        "near_grad" if part else "near_hidden",
        [((64, width), f32)] + [((64, width), bf16)] * 3,
        [whole, weight, far],
        scratch=[((256, tile), f32)],
        flops=2 * 256 * width * units,
        moved=6 * 2**20,
    )
    return mine, [to_y(send, step) for step, send in zip((1, 2, 3), sends)]


def on_device(inputs, w_in, w_out, grad_out):
    width, units = w_in.shape
    index = jnp.reshape(lax.axis_index("gz"), (1,)).astype(jnp.int32)
    steps = (1, 2, 3)
    (both,) = call(pair_kernel, "pair", [((32, width), bf16)], [inputs, grad_out], moved=2**18)
    columns = call(
        columns_kernel,
        "columns",
        [((64, width), bf16)] * 2,
        [both] + [from_gx(both, step) for step in steps],
        moved=2**20,
    )
    planes = [[column] + [from_y(column, step) for step in steps] for column in columns]
    near = halves(planes[0])
    width_flops = 2 * 512 * width * units
    all_inputs, own, *sends = call(
        width_inputs_kernel,
        "width_inputs",
        [((512, width), bf16), ((128, units), f32)] + [((128, units), bf16)] * 3,
        [index] + near + [other_core(piece) for piece in near] + [w_in],
        scratch=[((512, tile), f32)],
        flops=width_flops,
        moved=6 * 2**20,
        scalars=1,
    )
    mine, send = call(
        sum_x_kernel,
        "sum_x",
        [((64, units), f32)] * 2,
        [index, own] + [to_x(send, step) for step, send in zip(steps, sends)],
        moved=2**20,
        scalars=1,
    )
    hidden, slope = call(
        activation_kernel,
        "activation",
        [((64, units), bf16), ((64, units), f32)],
        [mine, other_z(send)],
        moved=2**20,
    )
    near = halves(planes[1])
    all_grads, own, send = call(
        width_grad_kernel,
        "width_grad",
        [((512, width), bf16), ((256, units), f32), ((256, units), bf16)],
        [index] + near + [other_core(piece) for piece in near] + [w_out],
        scratch=[((512, tile), f32)],
        flops=width_flops,
        moved=6 * 2**20,
        scalars=1,
    )
    mine, *sends = call(
        sum_z_kernel,
        "sum_z",
        [((64, units), f32)] + [((64, units), bf16)] * 3,
        [own, other_z(send)],
        moved=2**20,
    )
    (pair,) = call(
        pair_z_kernel,
        "pair_z",
        [((128, units), bf16)],
        [index, hidden, other_z(hidden)],
        moved=2**19,
        scalars=1,
    )
    (grad_pre,) = call(
        grad_pre_kernel,
        "grad_pre",
        [((64, units), bf16)],
        [mine] + [to_x(send, step) for step, send in zip(steps, sends)] + [slope],
        moved=2**20,
    )
    hidden_pieces = [pair] + [from_x(pair, step) for step in steps]
    grad_stack = stack([grad_pre] + [from_x(grad_pre, step) for step in steps], "grad_stack")
    hidden_all, far_hidden = units_far(
        far_hidden_kernel, "far_hidden", index, hidden_pieces, w_out, False
    )
    grad_pre_all, far_grad = units_far(
        far_grad_kernel, "far_grad", index, [grad_stack, other_z(grad_stack)], w_in, True
    )
    mine_hidden, parts_hidden = units_near(0, hidden_all, w_out, far_hidden)
    mine_grad, parts_grad = units_near(1, grad_pre_all, w_in, far_grad)
    grad_w_out = lax.dot_general(
        hidden_all, all_grads, (((0,), (0,)), ((), ())), preferred_element_type=f32
    ).astype(bf16)
    grad_w_in = lax.dot_general(
        all_inputs, grad_pre_all, (((0,), (0,)), ((), ())), preferred_element_type=f32
    ).astype(bf16)
    parts_hidden, grad_w_out = barrier((parts_hidden, grad_w_out))
    mine_hidden, ends_hidden = column_sum(mine_hidden, parts_hidden)
    mine_grad, ends_grad = column_sum(mine_grad, parts_grad)
    ends_hidden, mine_grad = barrier((ends_hidden, mine_grad))
    output = last_sum(mine_hidden, ends_hidden)
    grad_inputs = last_sum(mine_grad, ends_grad)
    return (output, grad_inputs, grad_w_in, grad_w_out)


def solution(mesh):
    in_specs = (
        P(("gx", "gy"), "gz"),
        P("gz", ("gx", "gy")),
        P(("gx", "gy"), "gz"),
        P(("gx", "gy"), "gz"),
    )
    out_specs = (
        P(("gx", "gy"), "gz"),
        P(("gx", "gy"), "gz"),
        P("gz", ("gx", "gy")),
        P(("gx", "gy"), "gz"),
    )
    return jax.shard_map(
        on_device, mesh=mesh, in_specs=in_specs, out_specs=out_specs, check_vma=False
    )
```

```python
import functools

import jax
import jax.numpy as jnp
from jax import lax
from jax.experimental import pallas as pl
from jax.experimental.pallas import tpu as pltpu
from jax.sharding import PartitionSpec as P

gelu_scale = 0.7978845608028654
cubic_term = 0.044715
tile = 256
bf16 = jnp.bfloat16
f32 = jnp.float32


def gelu_parts(value):
    inner = gelu_scale * (value + cubic_term * value * value * value)
    tanh_part = jnp.tanh(inner)
    result = 0.5 * value * (1.0 + tanh_part)
    slope = 0.5 * (1.0 + tanh_part) + 0.5 * value * (1.0 - tanh_part * tanh_part) * gelu_scale * (
        1.0 + 3.0 * cubic_term * value * value
    )
    return (result, slope)


barrier = lax.optimization_barrier


def swap_gx(value, step):
    return lax.ppermute(value, "gx", [(i, i ^ step) for i in range(4)])


def other_core(value):
    return lax.ppermute(value, "gy", [(i, i ^ 1) for i in range(8)])


def swap_y(value, step):
    return lax.ppermute(value, "gy", [(i, i ^ (2 * step)) for i in range(8)])


def swap_x(value, step):
    return lax.ppermute(value, "gz", [(i, i ^ (2 * step)) for i in range(8)])


def other_z(value):
    return lax.ppermute(value, "gz", [(i, i ^ 1) for i in range(8)])


def product(left, right, transposed):
    dims = (((1,), (1,)), ((), ())) if transposed else (((1,), (0,)), ((), ()))
    return lax.dot_general(left, right, dims, preferred_element_type=f32)


def columns_of(weight_ref, start, transposed):
    if transposed:
        return weight_ref[pl.ds(start, tile), :]
    return weight_ref[:, pl.ds(start, tile)]


def call(kernel, name, outs, args, scratch=(), flops=0, moved=0, scalars=0, aliases=None):
    vmem = pl.BlockSpec(memory_space=pltpu.VMEM)
    return pl.pallas_call(
        kernel,
        out_shape=[jax.ShapeDtypeStruct(*out) for out in outs],
        in_specs=[pl.BlockSpec(memory_space=pltpu.SMEM)] * scalars + [vmem] * (len(args) - scalars),
        out_specs=[vmem] * len(outs),
        scratch_shapes=[pltpu.VMEM(*shape) for shape in scratch],
        input_output_aliases=aliases or {},
        compiler_params=pltpu.CompilerParams(vmem_limit_bytes=8 * 2**20),
        cost_estimate=pl.CostEstimate(flops=flops, bytes_accessed=moved, transcendentals=0),
        name=name,
    )(*args)


def pair_kernel(inputs_ref, grads_ref, both_ref):
    both_ref[:16, :] = inputs_ref[...]
    both_ref[16:, :] = grads_ref[...]


def columns_kernel(both_ref, first_ref, second_ref, third_ref, inputs_ref, grads_ref):
    for i, source in enumerate((both_ref, first_ref, second_ref, third_ref)):
        inputs_ref[16 * i : 16 * i + 16, :] = source[:16, :]
        grads_ref[16 * i : 16 * i + 16, :] = source[16:, :]


def stack_kernel(*refs):
    rows = refs[0].shape[0]
    for i, piece in enumerate(refs[:4]):
        refs[4][rows * i : rows * (i + 1), :] = piece[...]


def stack(pieces, name):
    rows, width = pieces[0].shape
    return call(stack_kernel, name, [((4 * rows, width), bf16)], pieces, moved=2**20)[0]


def halves_kernel(*refs):
    for i, piece in enumerate(refs[:4]):
        refs[4 + i // 2][64 * (i % 2) : 64 * (i % 2) + 64, :] = piece[...]


def halves(pieces):
    width = pieces[0].shape[1]
    return list(call(halves_kernel, "plane", [((128, width), bf16)] * 2, pieces, moved=2**20))


def place(index_ref):
    me = index_ref[0]
    return lax.shift_right_logical(me, 1), lax.bitwise_and(me, 1)


def block(x, step, size, offset=0):
    return pl.ds(pl.multiple_of(lax.bitwise_xor(x, step) * 128 + offset, 64), size)


def width_inputs_kernel(index_ref, *refs):
    pieces, weight_ref = refs[:4], refs[4]
    whole_ref, own_ref, sends, acc = refs[5], refs[6], refs[7:10], refs[10]
    x, z = place(index_ref)
    for i, piece in enumerate(pieces):
        whole_ref[128 * i : 128 * i + 128, :] = piece[...]

    @pl.loop(0, own_ref.shape[1] // tile)
    def _(j):
        start = pl.multiple_of(j * tile, tile)
        cols = pl.ds(start, tile)
        acc[...] = product(whole_ref[...], columns_of(weight_ref, start, False), False)
        own_ref[:, cols] = acc[block(x, 0, 128), :]
        for step in (1, 2, 3):
            sends[step - 1][:, cols] = acc[block(x, step, 128), :].astype(bf16)


def width_grad_kernel(index_ref, *refs):
    pieces, weight_ref = refs[:4], refs[4]
    whole_ref, own_ref, send_ref, acc = refs[5:]
    x, z = place(index_ref)
    for i, piece in enumerate(pieces):
        whole_ref[128 * i : 128 * i + 128, :] = piece[...]

    @pl.loop(0, own_ref.shape[1] // tile)
    def _(j):
        start = pl.multiple_of(j * tile, tile)
        cols = pl.ds(start, tile)
        acc[...] = product(whole_ref[...], columns_of(weight_ref, start, True), True)
        for step in range(4):
            rows = slice(64 * step, 64 * step + 64)
            own_ref[rows, cols] = acc[block(x, step, 64, 64 * z), :]
            send_ref[rows, cols] = acc[block(x, step, 64, 64 * (1 - z)), :].astype(bf16)


def sum_x_kernel(index_ref, own_ref, first_ref, second_ref, third_ref, mine_ref, send_ref):
    x, z = place(index_ref)
    for target, half in ((mine_ref, z), (send_ref, 1 - z)):

        @pl.loop(0, 4)
        def _(j):
            rows = pl.ds(pl.multiple_of(64 * half + 16 * j, 16), 16)
            total = own_ref[rows, :]
            for piece in (first_ref, second_ref, third_ref):
                total = total + piece[rows, :].astype(f32)
            target[pl.ds(pl.multiple_of(16 * j, 16), 16), :] = total


def activation_kernel(mine_ref, part_ref, hidden_ref, slope_ref):
    @pl.loop(0, 4)
    def _(j):
        rows = pl.ds(pl.multiple_of(16 * j, 16), 16)
        result, slope = gelu_parts(mine_ref[rows, :] + part_ref[rows, :])
        hidden_ref[rows, :] = result.astype(bf16)
        slope_ref[rows, :] = slope


def sum_z_kernel(own_ref, part_ref, mine_ref, *sends):
    for step in range(4):

        @pl.loop(0, 4)
        def _(j):
            rows = pl.ds(pl.multiple_of(64 * step + 16 * j, 16), 16)
            local = pl.ds(pl.multiple_of(16 * j, 16), 16)
            total = own_ref[rows, :] + part_ref[rows, :].astype(f32)
            if step == 0:
                mine_ref[local, :] = total
            else:
                sends[step - 1][local, :] = total.astype(bf16)


def grad_pre_kernel(mine_ref, first_ref, second_ref, third_ref, slope_ref, out_ref):
    @pl.loop(0, 4)
    def _(j):
        rows = pl.ds(pl.multiple_of(16 * j, 16), 16)
        total = mine_ref[rows, :]
        for piece in (first_ref, second_ref, third_ref):
            total = total + piece[rows, :].astype(f32)
        out_ref[rows, :] = (total * slope_ref[rows, :]).astype(bf16)


def pair_z_kernel(index_ref, own_ref, part_ref, out_ref):
    x, z = place(index_ref)
    out_ref[pl.ds(pl.multiple_of(64 * z, 64), 64), :] = own_ref[...]
    out_ref[pl.ds(pl.multiple_of(64 * (1 - z), 64), 64), :] = part_ref[...]


def far_columns(whole_ref, weight_ref, far_ref, transposed):
    @pl.loop(0, far_ref.shape[1] // tile)
    def _(j):
        start = pl.multiple_of(j * tile, tile)
        far_ref[:, pl.ds(start, tile)] = product(
            whole_ref[256:, :], columns_of(weight_ref, start, transposed), transposed
        )


def far_hidden_kernel(index_ref, *refs):
    pieces, weight_ref, whole_ref, far_ref = refs[:4], refs[4], refs[5], refs[6]
    x, z = place(index_ref)
    for step in range(4):
        whole_ref[block(x, step, 128), :] = pieces[step][...]
    far_columns(whole_ref, weight_ref, far_ref, False)


def far_grad_kernel(index_ref, own_ref, part_ref, weight_ref, whole_ref, far_ref):
    x, z = place(index_ref)
    for step in range(4):
        rows = slice(64 * step, 64 * step + 64)
        whole_ref[block(x, step, 64, 64 * z), :] = own_ref[rows, :]
        whole_ref[block(x, step, 64, 64 * (1 - z)), :] = part_ref[rows, :]
    far_columns(whole_ref, weight_ref, far_ref, True)


def near_kernel(transposed, whole_ref, weight_ref, far_ref, mine_ref, *refs):
    sends, acc = refs[:3], refs[3]

    @pl.loop(0, mine_ref.shape[1] // tile)
    def _(j):
        start = pl.multiple_of(j * tile, tile)
        cols = pl.ds(start, tile)
        acc[...] = far_ref[:, cols] + product(
            whole_ref[:256, :], columns_of(weight_ref, start, transposed), transposed
        )
        mine_ref[:, cols] = acc[:64, :]
        for step in (1, 2, 3):
            sends[step - 1][:, cols] = acc[64 * step : 64 * step + 64, :].astype(bf16)


def column_kernel(*refs):
    mine_ref, sends = refs[4], refs[5:8]
    for step in range(4):
        rows = slice(16 * step, 16 * step + 16)
        total = refs[0][rows, :]
        for piece in refs[1:4]:
            total = total + piece[rows, :].astype(f32)
        if step == 0:
            mine_ref[...] = total
        else:
            sends[step - 1][...] = total.astype(bf16)


def last_kernel(mine_ref, first_ref, second_ref, third_ref, out_ref):
    total = mine_ref[...]
    for piece in (first_ref, second_ref, third_ref):
        total = total + piece[...].astype(f32)
    out_ref[...] = total.astype(bf16)


def column_sum(mine, parts):
    width = mine.shape[1]
    mine, *sends = call(
        column_kernel,
        "column_sum",
        [((16, width), f32)] + [((16, width), bf16)] * 3,
        [mine] + list(parts),
        moved=2**20,
    )
    return mine, [swap_gx(send, step) for step, send in zip((1, 2, 3), sends)]


def last_sum(mine, parts):
    return call(last_kernel, "last_sum", [(mine.shape, bf16)], [mine] + list(parts), moved=2**18)[0]


def units_far(kernel, name, index, pieces, weight, transposed):
    units = pieces[0].shape[1]
    width = weight.shape[0] if transposed else weight.shape[1]
    whole, far = call(
        kernel,
        name,
        [((512, units), bf16), ((256, width), f32)],
        [index] + pieces + [weight],
        flops=2 * 256 * width * units,
        moved=6 * 2**20,
        scalars=1,
    )
    return whole, other_core(far)


def units_near(part, whole, weight, far):
    units, width = whole.shape[1], far.shape[1]
    mine, *sends = call(
        functools.partial(near_kernel, bool(part)),
        "near_grad" if part else "near_hidden",
        [((64, width), f32)] + [((64, width), bf16)] * 3,
        [whole, weight, far],
        scratch=[((256, tile), f32)],
        flops=2 * 256 * width * units,
        moved=6 * 2**20,
    )
    return mine, [swap_y(send, step) for step, send in zip((1, 2, 3), sends)]


def on_device(inputs, w_in, w_out, grad_out):
    width, units = w_in.shape
    index = jnp.reshape(lax.axis_index("gz"), (1,)).astype(jnp.int32)
    steps = (1, 2, 3)
    (both,) = call(pair_kernel, "pair", [((32, width), bf16)], [inputs, grad_out], moved=2**18)
    columns = call(
        columns_kernel,
        "columns",
        [((64, width), bf16)] * 2,
        [both] + [swap_gx(both, step) for step in steps],
        moved=2**20,
    )
    planes = [[column] + [swap_y(column, step) for step in steps] for column in columns]
    near = halves(planes[0])
    width_flops = 2 * 512 * width * units
    all_inputs, own, *sends = call(
        width_inputs_kernel,
        "width_inputs",
        [((512, width), bf16), ((128, units), f32)] + [((128, units), bf16)] * 3,
        [index] + near + [other_core(piece) for piece in near] + [w_in],
        scratch=[((512, tile), f32)],
        flops=width_flops,
        moved=6 * 2**20,
        scalars=1,
    )
    mine, send = call(
        sum_x_kernel,
        "sum_x",
        [((64, units), f32)] * 2,
        [index, own] + [swap_x(send, step) for step, send in zip(steps, sends)],
        moved=2**20,
        scalars=1,
    )
    hidden, slope = call(
        activation_kernel,
        "activation",
        [((64, units), bf16), ((64, units), f32)],
        [mine, other_z(send)],
        moved=2**20,
    )
    near = halves(planes[1])
    all_grads, own, send = call(
        width_grad_kernel,
        "width_grad",
        [((512, width), bf16), ((256, units), f32), ((256, units), bf16)],
        [index] + near + [other_core(piece) for piece in near] + [w_out],
        scratch=[((512, tile), f32)],
        flops=width_flops,
        moved=6 * 2**20,
        scalars=1,
    )
    mine, *sends = call(
        sum_z_kernel,
        "sum_z",
        [((64, units), f32)] + [((64, units), bf16)] * 3,
        [own, other_z(send)],
        moved=2**20,
    )
    (pair,) = call(
        pair_z_kernel,
        "pair_z",
        [((128, units), bf16)],
        [index, hidden, other_z(hidden)],
        moved=2**19,
        scalars=1,
    )
    (grad_pre,) = call(
        grad_pre_kernel,
        "grad_pre",
        [((64, units), bf16)],
        [mine] + [swap_x(send, step) for step, send in zip(steps, sends)] + [slope],
        moved=2**20,
    )
    hidden_pieces = [pair] + [swap_x(pair, step) for step in steps]
    grad_stack = stack([grad_pre] + [swap_x(grad_pre, step) for step in steps], "grad_stack")
    hidden_all, far_hidden = units_far(
        far_hidden_kernel, "far_hidden", index, hidden_pieces, w_out, False
    )
    grad_pre_all, far_grad = units_far(
        far_grad_kernel, "far_grad", index, [grad_stack, other_z(grad_stack)], w_in, True
    )
    mine_hidden, parts_hidden = units_near(0, hidden_all, w_out, far_hidden)
    mine_grad, parts_grad = units_near(1, grad_pre_all, w_in, far_grad)
    grad_w_out = lax.dot_general(
        hidden_all, all_grads, (((0,), (0,)), ((), ())), preferred_element_type=f32
    ).astype(bf16)
    grad_w_in = lax.dot_general(
        all_inputs, grad_pre_all, (((0,), (0,)), ((), ())), preferred_element_type=f32
    ).astype(bf16)
    parts_hidden, grad_w_out = barrier((parts_hidden, grad_w_out))
    mine_hidden, ends_hidden = column_sum(mine_hidden, parts_hidden)
    mine_grad, ends_grad = column_sum(mine_grad, parts_grad)
    ends_hidden, mine_grad = barrier((ends_hidden, mine_grad))
    output = last_sum(mine_hidden, ends_hidden)
    grad_inputs = last_sum(mine_grad, ends_grad)
    return (output, grad_inputs, grad_w_in, grad_w_out)


def solution(mesh):
    in_specs = (
        P(("gx", "gy"), "gz"),
        P("gz", ("gx", "gy")),
        P(("gx", "gy"), "gz"),
        P(("gx", "gy"), "gz"),
    )
    out_specs = (
        P(("gx", "gy"), "gz"),
        P(("gx", "gy"), "gz"),
        P("gz", ("gx", "gy")),
        P(("gx", "gy"), "gz"),
    )
    return jax.shard_map(
        on_device, mesh=mesh, in_specs=in_specs, out_specs=out_specs, check_vma=False
    )
```

```python
import functools

import jax
import jax.numpy as jnp
from jax import lax
from jax.experimental import pallas as pl
from jax.experimental.pallas import tpu as pltpu
from jax.sharding import PartitionSpec as P

gelu_scale = 0.7978845608028654
cubic_term = 0.044715
tile = 256
bf16 = jnp.bfloat16
f32 = jnp.float32


def gelu_parts(value):
    inner = gelu_scale * (value + cubic_term * value * value * value)
    tanh_part = jnp.tanh(inner)
    result = 0.5 * value * (1.0 + tanh_part)
    slope = 0.5 * (1.0 + tanh_part) + 0.5 * value * (1.0 - tanh_part * tanh_part) * gelu_scale * (
        1.0 + 3.0 * cubic_term * value * value
    )
    return (result, slope)


barrier = lax.optimization_barrier


def from_gx(value, step):
    return lax.ppermute(value, "gx", [((i + step) % 4, i) for i in range(4)])


def to_gx(value, step):
    return lax.ppermute(value, "gx", [(i, (i + step) % 4) for i in range(4)])


def other_core(value):
    return lax.ppermute(value, "gy", [(i, i ^ 1) for i in range(8)])


def from_y(value, step):
    return lax.ppermute(value, "gy", [((i + 2 * step) % 8, i) for i in range(8)])


def to_y(value, step):
    return lax.ppermute(value, "gy", [(i, (i + 2 * step) % 8) for i in range(8)])


def from_x(value, step):
    return lax.ppermute(value, "gz", [((i + 2 * step) % 8, i) for i in range(8)])


def to_x(value, step):
    return lax.ppermute(value, "gz", [(i, (i + 2 * step) % 8) for i in range(8)])


def other_z(value):
    return lax.ppermute(value, "gz", [(i, i ^ 1) for i in range(8)])


def product(left, right, transposed):
    dims = (((1,), (1,)), ((), ())) if transposed else (((1,), (0,)), ((), ()))
    return lax.dot_general(left, right, dims, preferred_element_type=f32)


def columns_of(weight_ref, start, transposed):
    if transposed:
        return weight_ref[pl.ds(start, tile), :]
    return weight_ref[:, pl.ds(start, tile)]


def call(kernel, name, outs, args, scratch=(), flops=0, moved=0, scalars=0, aliases=None):
    vmem = pl.BlockSpec(memory_space=pltpu.VMEM)
    return pl.pallas_call(
        kernel,
        out_shape=[jax.ShapeDtypeStruct(*out) for out in outs],
        in_specs=[pl.BlockSpec(memory_space=pltpu.SMEM)] * scalars + [vmem] * (len(args) - scalars),
        out_specs=[vmem] * len(outs),
        scratch_shapes=[pltpu.VMEM(*shape) for shape in scratch],
        input_output_aliases=aliases or {},
        compiler_params=pltpu.CompilerParams(vmem_limit_bytes=8 * 2**20),
        cost_estimate=pl.CostEstimate(flops=flops, bytes_accessed=moved, transcendentals=0),
        name=name,
    )(*args)


def pair_kernel(inputs_ref, grads_ref, both_ref):
    both_ref[:16, :] = inputs_ref[...]
    both_ref[16:, :] = grads_ref[...]


def columns_kernel(both_ref, first_ref, second_ref, third_ref, inputs_ref, grads_ref):
    for i, source in enumerate((both_ref, first_ref, second_ref, third_ref)):
        inputs_ref[16 * i : 16 * i + 16, :] = source[:16, :]
        grads_ref[16 * i : 16 * i + 16, :] = source[16:, :]


def stack_kernel(*refs):
    rows = refs[0].shape[0]
    for i, piece in enumerate(refs[:4]):
        refs[4][rows * i : rows * (i + 1), :] = piece[...]


def stack(pieces, name):
    rows, width = pieces[0].shape
    return call(stack_kernel, name, [((4 * rows, width), bf16)], pieces, moved=2**20)[0]


def halves_kernel(*refs):
    for i, piece in enumerate(refs[:4]):
        refs[i // 2 - 2][64 * (i % 2) : 64 * (i % 2) + 64, :] = piece[...]


def halves(pieces):
    width = pieces[0].shape[1]
    return list(call(halves_kernel, "plane", [((128, width), bf16)] * 2, pieces, moved=2**20))


def place(index_ref):
    me = index_ref[0]
    return lax.shift_right_logical(me, 1), lax.bitwise_and(me, 1)


def block(x, step, size, offset=0):
    return pl.ds(pl.multiple_of(lax.bitwise_and(x + step, 3) * 128 + offset, 64), size)


def width_inputs_kernel(index_ref, *refs):
    pieces, weight_ref = refs[:4], refs[4]
    whole_ref, own_ref, sends, acc = refs[5], refs[6], refs[7:10], refs[10]
    x, z = place(index_ref)
    for i, piece in enumerate(pieces):
        whole_ref[128 * i : 128 * i + 128, :] = piece[...]

    @pl.loop(0, own_ref.shape[1] // tile)
    def _(j):
        start = pl.multiple_of(j * tile, tile)
        cols = pl.ds(start, tile)
        acc[...] = product(whole_ref[...], columns_of(weight_ref, start, False), False)
        own_ref[:, cols] = acc[block(x, 0, 128), :]
        for step in (1, 2, 3):
            sends[step - 1][:, cols] = acc[block(x, step, 128), :].astype(bf16)


def width_grad_kernel(index_ref, *refs):
    pieces, weight_ref = refs[:4], refs[4]
    whole_ref, own_ref, send_ref, acc = refs[5:]
    x, z = place(index_ref)
    for i, piece in enumerate(pieces):
        whole_ref[128 * i : 128 * i + 128, :] = piece[...]

    @pl.loop(0, own_ref.shape[1] // tile)
    def _(j):
        start = pl.multiple_of(j * tile, tile)
        cols = pl.ds(start, tile)
        acc[...] = product(whole_ref[...], columns_of(weight_ref, start, True), True)
        for step in range(4):
            rows = slice(64 * step, 64 * step + 64)
            own_ref[rows, cols] = acc[block(x, step, 64, 64 * z), :]
            send_ref[rows, cols] = acc[block(x, step, 64, 64 * (1 - z)), :].astype(bf16)


def sum_x_kernel(index_ref, own_ref, first_ref, second_ref, third_ref, mine_ref, send_ref):
    x, z = place(index_ref)
    for target, half in ((mine_ref, z), (send_ref, 1 - z)):

        @pl.loop(0, 4)
        def _(j):
            rows = pl.ds(pl.multiple_of(64 * half + 16 * j, 16), 16)
            total = own_ref[rows, :]
            for piece in (first_ref, second_ref, third_ref):
                total = total + piece[rows, :].astype(f32)
            target[pl.ds(pl.multiple_of(16 * j, 16), 16), :] = total


def activation_kernel(mine_ref, part_ref, hidden_ref, slope_ref):
    @pl.loop(0, 4)
    def _(j):
        rows = pl.ds(pl.multiple_of(16 * j, 16), 16)
        result, slope = gelu_parts(mine_ref[rows, :] + part_ref[rows, :])
        hidden_ref[rows, :] = result.astype(bf16)
        slope_ref[rows, :] = slope


def sum_z_kernel(own_ref, part_ref, mine_ref, *sends):
    for step in range(4):

        @pl.loop(0, 4)
        def _(j):
            rows = pl.ds(pl.multiple_of(64 * step + 16 * j, 16), 16)
            local = pl.ds(pl.multiple_of(16 * j, 16), 16)
            total = own_ref[rows, :] + part_ref[rows, :].astype(f32)
            if step == 0:
                mine_ref[local, :] = total
            else:
                sends[step - 1][local, :] = total.astype(bf16)


def grad_pre_kernel(mine_ref, first_ref, second_ref, third_ref, slope_ref, out_ref):
    @pl.loop(0, 4)
    def _(j):
        rows = pl.ds(pl.multiple_of(16 * j, 16), 16)
        total = mine_ref[rows, :]
        for piece in (first_ref, second_ref, third_ref):
            total = total + piece[rows, :].astype(f32)
        out_ref[rows, :] = (total * slope_ref[rows, :]).astype(bf16)


def pair_z_kernel(index_ref, own_ref, part_ref, out_ref):
    x, z = place(index_ref)
    out_ref[pl.ds(pl.multiple_of(64 * z, 64), 64), :] = own_ref[...]
    out_ref[pl.ds(pl.multiple_of(64 * (1 - z), 64), 64), :] = part_ref[...]


def far_columns(whole_ref, weight_ref, far_ref, transposed):
    @pl.loop(0, far_ref.shape[1] // tile)
    def _(j):
        start = pl.multiple_of(j * tile, tile)
        far_ref[:, pl.ds(start, tile)] = product(
            whole_ref[256:, :], columns_of(weight_ref, start, transposed), transposed
        )


def far_hidden_kernel(index_ref, *refs):
    pieces, weight_ref, whole_ref, far_ref = refs[:4], refs[4], refs[5], refs[6]
    x, z = place(index_ref)
    for step in range(4):
        whole_ref[block(x, step, 128), :] = pieces[step][...]
    far_columns(whole_ref, weight_ref, far_ref, False)


def far_grad_kernel(index_ref, own_ref, part_ref, weight_ref, whole_ref, far_ref):
    x, z = place(index_ref)
    for step in range(4):
        rows = slice(64 * step, 64 * step + 64)
        whole_ref[block(x, step, 64, 64 * z), :] = own_ref[rows, :]
        whole_ref[block(x, step, 64, 64 * (1 - z)), :] = part_ref[rows, :]
    far_columns(whole_ref, weight_ref, far_ref, True)


def near_kernel(transposed, whole_ref, weight_ref, far_ref, mine_ref, *refs):
    sends, acc = refs[:3], refs[3]

    @pl.loop(0, mine_ref.shape[1] // tile)
    def _(j):
        start = pl.multiple_of(j * tile, tile)
        cols = pl.ds(start, tile)
        acc[...] = far_ref[:, cols] + product(
            whole_ref[:256, :], columns_of(weight_ref, start, transposed), transposed
        )
        mine_ref[:, cols] = acc[:64, :]
        for step in (1, 2, 3):
            sends[step - 1][:, cols] = acc[64 * step : 64 * step + 64, :].astype(bf16)


def column_kernel(*refs):
    mine_ref, sends = refs[4], refs[5:8]
    for step in range(4):
        rows = slice(16 * step, 16 * step + 16)
        total = refs[0][rows, :]
        for piece in refs[1:4]:
            total = total + piece[rows, :].astype(f32)
        if step == 0:
            mine_ref[...] = total
        else:
            sends[step - 1][...] = total.astype(bf16)


def last_kernel(*refs):
    for part in range(2):
        total = refs[4 * part][...]
        for piece in refs[4 * part + 1 : 4 * part + 4]:
            total = total + piece[...].astype(f32)
        refs[8 + part][...] = total.astype(bf16)


def column_sum(mine, parts):
    width = mine.shape[1]
    mine, *sends = call(
        column_kernel,
        "column_sum",
        [((16, width), f32)] + [((16, width), bf16)] * 3,
        [mine] + list(parts),
        moved=2**20,
    )
    return mine, [to_gx(send, step) for step, send in zip((1, 2, 3), sends)]


def units_far(kernel, name, index, pieces, weight, transposed):
    units = pieces[0].shape[1]
    width = weight.shape[0] if transposed else weight.shape[1]
    whole, far = call(
        kernel,
        name,
        [((512, units), bf16), ((256, width), f32)],
        [index] + pieces + [weight],
        flops=2 * 256 * width * units,
        moved=6 * 2**20,
        scalars=1,
    )
    return whole, other_core(far)


def units_near(part, whole, weight, far):
    units, width = whole.shape[1], far.shape[1]
    mine, *sends = call(
        functools.partial(near_kernel, bool(part)),
        "near_grad" if part else "near_hidden",
        [((64, width), f32)] + [((64, width), bf16)] * 3,
        [whole, weight, far],
        scratch=[((256, tile), f32)],
        flops=2 * 256 * width * units,
        moved=6 * 2**20,
    )
    return mine, [to_y(send, step) for step, send in zip((1, 2, 3), sends)]


def on_device(inputs, w_in, w_out, grad_out):
    width, units = w_in.shape
    index = jnp.reshape(lax.axis_index("gz"), (1,)).astype(jnp.int32)
    steps = (1, 2, 3)
    (both,) = call(pair_kernel, "pair", [((32, width), bf16)], [inputs, grad_out], moved=2**18)
    columns = call(
        columns_kernel,
        "columns",
        [((64, width), bf16)] * 2,
        [both] + [from_gx(both, step) for step in steps],
        moved=2**20,
    )
    planes = [[column] + [from_y(column, step) for step in steps] for column in columns]
    near = halves(planes[0])
    width_flops = 2 * 512 * width * units
    all_inputs, own, *sends = call(
        width_inputs_kernel,
        "width_inputs",
        [((512, width), bf16), ((128, units), f32)] + [((128, units), bf16)] * 3,
        [index] + near + [other_core(piece) for piece in near] + [w_in],
        scratch=[((512, tile), f32)],
        flops=width_flops,
        moved=6 * 2**20,
        scalars=1,
    )
    mine, send = call(
        sum_x_kernel,
        "sum_x",
        [((64, units), f32)] * 2,
        [index, own] + [to_x(send, step) for step, send in zip(steps, sends)],
        moved=2**20,
        scalars=1,
    )
    hidden, slope = call(
        activation_kernel,
        "activation",
        [((64, units), bf16), ((64, units), f32)],
        [mine, other_z(send)],
        moved=2**20,
    )
    near = halves(planes[1])
    all_grads, own, send = call(
        width_grad_kernel,
        "width_grad",
        [((512, width), bf16), ((256, units), f32), ((256, units), bf16)],
        [index] + near + [other_core(piece) for piece in near] + [w_out],
        scratch=[((512, tile), f32)],
        flops=width_flops,
        moved=6 * 2**20,
        scalars=1,
    )
    mine, *sends = call(
        sum_z_kernel,
        "sum_z",
        [((64, units), f32)] + [((64, units), bf16)] * 3,
        [own, other_z(send)],
        moved=2**20,
    )
    (pair,) = call(
        pair_z_kernel,
        "pair_z",
        [((128, units), bf16)],
        [index, hidden, other_z(hidden)],
        moved=2**19,
        scalars=1,
    )
    (grad_pre,) = call(
        grad_pre_kernel,
        "grad_pre",
        [((64, units), bf16)],
        [mine] + [to_x(send, step) for step, send in zip(steps, sends)] + [slope],
        moved=2**20,
    )
    hidden_pieces = [pair] + [from_x(pair, step) for step in steps]
    grad_stack = stack([grad_pre] + [from_x(grad_pre, step) for step in steps], "grad_stack")
    hidden_all, far_hidden = units_far(
        far_hidden_kernel, "far_hidden", index, hidden_pieces, w_out, False
    )
    grad_pre_all, far_grad = units_far(
        far_grad_kernel, "far_grad", index, [grad_stack, other_z(grad_stack)], w_in, True
    )
    mine_hidden, parts_hidden = units_near(0, hidden_all, w_out, far_hidden)
    mine_grad, parts_grad = units_near(1, grad_pre_all, w_in, far_grad)
    grad_w_out = lax.dot_general(
        hidden_all, all_grads, (((0,), (0,)), ((), ())), preferred_element_type=f32
    ).astype(bf16)
    grad_w_in = lax.dot_general(
        all_inputs, grad_pre_all, (((0,), (0,)), ((), ())), preferred_element_type=f32
    ).astype(bf16)
    parts_hidden, grad_w_out = barrier((parts_hidden, grad_w_out))
    mine_hidden, ends_hidden = column_sum(mine_hidden, parts_hidden)
    mine_grad, ends_grad = column_sum(mine_grad, parts_grad)
    output, grad_inputs = call(
        last_kernel,
        "last_sums",
        [((16, width), bf16)] * 2,
        [mine_hidden] + ends_hidden + [mine_grad] + ends_grad,
        moved=2**19,
    )
    return (output, grad_inputs, grad_w_in, grad_w_out)


def solution(mesh):
    in_specs = (
        P(("gx", "gy"), "gz"),
        P("gz", ("gx", "gy")),
        P(("gx", "gy"), "gz"),
        P(("gx", "gy"), "gz"),
    )
    out_specs = (
        P(("gx", "gy"), "gz"),
        P(("gx", "gy"), "gz"),
        P("gz", ("gx", "gy")),
        P(("gx", "gy"), "gz"),
    )
    return jax.shard_map(
        on_device, mesh=mesh, in_specs=in_specs, out_specs=out_specs, check_vma=False
    )
```
